128 devices in a mesh: comp: 2 (over z_lo), tile: 64 (over x, y, z_hi, core).
Axes of the slice: x: 4, y: 4, z: 4 (z_hi: 2, z_lo: 2; z = z_hi * 2 + z_lo), core: 2. Of those that a mesh axis runs over, the one named last changes fastest.
Arguments:
- state: float32 [2, 4, 16, 16, 32768], P('comp', None, None, None, 'tile'), may hold values from -6 to 6
- metric: float32 [2, 32768], P('comp', 'tile'), may hold values from 0.5 to 2
- element_coupling: float32 [2, 16, 16], P('comp'), may hold values from -0.2 to 0.2
- level_coupling: float32 [2, 16, 16], P('comp'), may hold values from -0.2 to 0.2
- coeffs: float32 [2, 3], P('comp'), may hold values from 0.1 to 0.4
- edge_partner: int32 [2, 131072], P('comp', 'tile'), may hold values from 0 to 3071, as said below
- sea_mask: int32 [2, 16, 32768], P('comp', None, 'tile'), may hold values 0 or 1
- forcing: float32 [2, 4, 16, 32768], P('comp', None, None, 'tile'), may hold values from -6 to 6
- remap_weights: bfloat16 [2, 5120, 128, 128], P('comp', 'tile'), may hold values from -0.375 to 0.375
- remap_rows: int32 [2, 5120], P('comp', 'tile'), may hold values from 0 to 64, as said below
- remap_cols: int32 [2, 5120], P('comp', 'tile'), may hold values from 0 to 191
Outputs:
- state_next: float32 [2, 4, 16, 16, 32768], P('comp', None, None, None, 'tile')
- forcing_next: float32 [2, 4, 16, 32768], P('comp', None, None, 'tile')
The draws below stay inside these ranges and needn't reach their ends.
Inputs may be any that keep to these rules, and one draw needn't show every extreme that they name: `edge_partner`: edge slots are edge-major (slot e * 512 + k). The pairing is symmetric: slots 0 to 511 meet the previous tile's last 512 slots, the last 512 slots meet the next tile's first 512, all other slots meet slots of their own tile; no slot meets itself. `remap_rows`: within a tile every row block 0 to 63 has at least one slot; a slot holding 64 is unused and adds nothing; the number of used slots differs from tile to tile, and some tile uses all 80.
All inputs are finite; a program needn't handle non-finite values. No bound on the sum of `sea_mask` on one device may be relied on, other than what follows from the above.
Results may differ from the reference program's by a relative error of at most 0.0029.
Values may be sent and summed in bfloat16 or wider, within the bound.
No kernel may reach another device: no remote copies, remote signals or barrier semaphores. Data moves between devices by JAX's collectives and lax.ppermute only.
A program may use at most 192 MiB of HBM per device.

```python
import math
import jax
import jax.numpy as jnp
import numpy as np
from jax import lax

VAR = 4
LEV = 16
NODE = 16
BLK = 128
ELEM_DEV = 512
BND = 512
RB = 64
NB = 80
ELEMS = 32768
N_TILE = 64


def draw_edge_partner(key, part):
    key = jax.random.fold_in(key, 11)
    slots = 4 * ELEM_DEV
    middle = slots - 2 * BND

    def one_tile(number):
        tile_key = jax.random.fold_in(key, number)
        key_across, key_inside = jax.random.split(tile_key)
        across = jax.random.permutation(key_across, BND).astype(jnp.int32)
        inside = jax.random.permutation(key_inside, middle).astype(jnp.int32)
        return (across, inside)
    across, inside = jax.vmap(one_tile)(jnp.arange(2 * N_TILE, dtype=jnp.int32))
    across = across.reshape(2, N_TILE, BND)
    inside = inside.reshape(2, N_TILE, middle)
    inverse = jnp.argsort(across, axis=-1).astype(jnp.int32)
    upper = slots + BND + jnp.roll(inverse, -1, axis=1)
    firsts = inside[..., 0::2]
    seconds = inside[..., 1::2]

    def fill_pairs(first_one, second_one):
        paired_one = jnp.zeros((middle,), jnp.int32)
        paired_one = paired_one.at[first_one].set(second_one + 2 * BND)
        return paired_one.at[second_one].set(first_one + 2 * BND)
    paired = jax.vmap(jax.vmap(fill_pairs))(firsts, seconds)
    result = jnp.concatenate([across, paired, upper.astype(jnp.int32)], axis=-1)
    return result.reshape(2, N_TILE * slots)


def draw_remap_rows(key, part):
    key = jax.random.fold_in(key, 23)
    key_full, key_sparse, key_rest = jax.random.split(key, 3)
    full_tile = jax.random.randint(key_full, (2,), 0, N_TILE)
    sparse_tile = (full_tile + 1 + jax.random.randint(key_sparse, (2,), 0, N_TILE - 1)) % N_TILE

    def one_device(number):
        device_key = jax.random.fold_in(key_rest, number)
        key_used, key_extra, key_base, key_order = jax.random.split(device_key, 4)
        component = number // N_TILE
        position = number % N_TILE
        used = jax.random.randint(key_used, (), RB, NB + 1)
        used = jnp.where(position == full_tile[component], NB, jnp.where(position == sparse_tile[component], RB, used))
        extra = jax.random.randint(key_extra, (NB - RB,), 0, RB)
        base = jnp.concatenate([jax.random.permutation(key_base, RB).astype(jnp.int32), extra.astype(jnp.int32)])
        slot_numbers = jnp.arange(NB, dtype=jnp.int32)
        base = jnp.where(slot_numbers < used, base, RB)
        shuffle = jax.random.permutation(key_order, NB)
        return base[shuffle]
    rows = jax.vmap(one_device)(jnp.arange(2 * N_TILE, dtype=jnp.int32))
    return rows.reshape(2, N_TILE * NB).astype(jnp.int32)


def touch_ends(entries, stream_key, smallest, high):
    shape = entries.shape
    place = [jax.random.randint(jax.random.fold_in(stream_key, axis), (), 0, shape[axis]) for axis in range(len(shape))]
    entries = entries.at[tuple(place)].set(smallest)
    longest = shape.index(max(shape))
    place[longest] = (place[longest] + 1) % shape[longest]
    return entries.at[tuple(place)].set(high)


def block_scale(rng, extent, cuts, least, top_value):
    def one(axis_at, parts):
        draws = jax.random.uniform(jax.random.fold_in(jax.random.fold_in(rng, 6), axis_at), (parts,), jnp.float32, least / len(cuts), top_value / len(cuts))
        return jnp.repeat(jnp.exp(draws), extent[axis_at] // parts).reshape((-1,) + (1,) * (len(extent) - axis_at - 1))

    level = one(*cuts[0])
    for cut in cuts[1:]:
        level = level * one(*cut)
    return level


def centred(key, dims, deviation, most, shards=(), kind=jnp.bfloat16):
    values = deviation * jax.random.normal(key, dims, jnp.float32)
    if shards:
        values = values * block_scale(key, dims, shards, -0.22, 0.18)
    return jnp.clip(values, -most, most).astype(kind)


def setup_inputs(seed: int = 0) -> dict:
    arg_keys = jax.random.split(jax.random.key(seed), 12)
    return {
        "state": centred(arg_keys[0], (2, VAR, LEV, NODE, ELEMS), 1.0, 6.0, ((0, 2), (4, 64)), jnp.float32),
        "metric": jnp.clip(jnp.exp(math.log(2.0) - 1.3862944 * jax.random.uniform(arg_keys[1], (2, ELEMS), jnp.float32) ** block_scale(arg_keys[1], (2, ELEMS), ((0, 2), (1, 64)), -0.2, 0.2)), 0.5, 2.0),
        "element_coupling": centred(arg_keys[2], (2, NODE, NODE), 0.04, 0.2, ((0, 2),), jnp.float32),
        "level_coupling": centred(arg_keys[3], (2, LEV, LEV), 0.04, 0.2, ((0, 2),), jnp.float32),
        "coeffs": jnp.clip(0.1 + 0.3 * jax.random.uniform(arg_keys[4], (2, 3), jnp.float32) ** block_scale(arg_keys[4], (2, 3), ((0, 2),), -0.2, 0.2), 0.1, 0.4),
        "edge_partner": draw_edge_partner(jax.random.fold_in(arg_keys[11], 71), 0),
        "sea_mask": touch_ends((jax.random.randint(arg_keys[6], (2, NODE, ELEMS), 0, 3) < 2).astype(jnp.int32), jax.random.fold_in(arg_keys[6], 1), 0, 1),
        "forcing": centred(arg_keys[7], (2, VAR, NODE, ELEMS), 1.0, 6.0, ((0, 2), (3, 64)), jnp.float32),
        "remap_weights": centred(arg_keys[8], (2, N_TILE * NB, BLK, BLK), (2 * BLK) ** -0.5, 0.375, ((0, 2), (1, 64))),
        "remap_rows": draw_remap_rows(jax.random.fold_in(arg_keys[11], 71), 0),
        "remap_cols": touch_ends(jax.random.randint(arg_keys[10], (2, N_TILE * NB), 0, 3 * RB), jax.random.fold_in(arg_keys[10], 1), 0, (3 * RB) - 1).astype(jnp.int32),
    }


EDGE_NODES = np.array([[0, 1, 2, 3], [3, 7, 11, 15], [0, 4, 8, 12], [12, 13, 14, 15]], dtype=np.int32)
FLAT_NODES = EDGE_NODES.reshape(-1)
HIGHEST_PRECISION = lax.Precision.HIGHEST


def edge_values(values):
    picked = values[..., FLAT_NODES, :]
    leading = picked.shape[:-2]
    elements = picked.shape[-1]
    picked = jnp.swapaxes(picked.reshape(leading + (4, 4, elements)), -3, -2)
    return picked.reshape(leading + (4, 4 * elements))


def edge_spread(differ, node_count):
    leading = differ.shape[:-2]
    elements = differ.shape[-1] // 4
    pieces = jnp.swapaxes(differ.reshape(leading + (4, 4, elements)), -3, -2)
    pieces = pieces.reshape(leading + (16, elements))
    result = jnp.zeros(leading + (node_count, elements), jnp.float32)
    return result.at[..., FLAT_NODES, :].add(pieces)


def tendency(state_now, partner_edges, own_edges, metric, element_coupling, level_coupling, penalty, exchange_rate, forcing):
    node_count = state_now.shape[-2]
    level_count = state_now.shape[-3]
    node_matrix = element_coupling - 0.3 * jnp.eye(node_count, dtype=jnp.float32)
    level_matrix = level_coupling - 0.2 * jnp.eye(level_count, dtype=jnp.float32)
    across = jnp.einsum('nm,...mk->...nk', node_matrix, state_now, precision=HIGHEST_PRECISION)
    across = across * metric[..., None, None, None, :]
    upward = jnp.einsum('lm,...mnk->...lnk', level_matrix, state_now, precision=HIGHEST_PRECISION)
    coupling = penalty * edge_spread(partner_edges - own_edges, node_count)
    total = across + upward + coupling
    lowest = state_now[..., 0, :, :]
    return total.at[..., 0, :, :].add(exchange_rate[..., None, :, :] * (forcing - lowest))


def advance_component(state_comp, metric_comp, element_comp, level_comp, coeff_comp, partner_comp, mask_comp, forcing_comp):
    current = jnp.moveaxis(state_comp.reshape(VAR, LEV, NODE, N_TILE, ELEM_DEV), 3, 0)
    metric_tiles = metric_comp.reshape(N_TILE, ELEM_DEV)
    partner_tiles = partner_comp.reshape(N_TILE, 4 * ELEM_DEV)
    mask_tiles = jnp.moveaxis(mask_comp.reshape(NODE, N_TILE, ELEM_DEV), 1, 0).astype(jnp.float32)
    exchange_rate = coeff_comp[1] * mask_tiles + coeff_comp[2] * (1.0 - mask_tiles)
    forcing_tiles = jnp.moveaxis(forcing_comp.reshape(VAR, NODE, N_TILE, ELEM_DEV), 2, 0)
    for substep in range(2):
        own_edges = edge_values(current)
        below = jnp.roll(own_edges, 1, axis=0)[..., own_edges.shape[-1] - BND:]
        above = jnp.roll(own_edges, -1, axis=0)[..., :BND]
        extended = jnp.concatenate([below, own_edges, above], axis=-1)
        lookup = jnp.broadcast_to(partner_tiles[:, None, None, None, :], own_edges.shape)
        partner_edges = jnp.take_along_axis(extended, lookup, axis=-1)[..., ::-1, :]
        current = current + tendency(current, partner_edges, own_edges, metric_tiles, element_comp, level_comp, coeff_comp[0], exchange_rate, forcing_tiles)
    surface = current[:, :, 0].astype(jnp.bfloat16).reshape(N_TILE, VAR, NODE * ELEM_DEV)
    state_out = jnp.moveaxis(current, 0, 3).reshape(VAR, LEV, NODE, N_TILE * ELEM_DEV)
    return state_out, surface


def remap(source, weights_comp, rows_comp, cols_comp):
    below = jnp.roll(source, 1, axis=0)
    above = jnp.roll(source, -1, axis=0)
    window = jnp.concatenate([below, source, above], axis=-1).reshape(N_TILE, VAR, 3 * RB, BLK)
    blocks = weights_comp.reshape(N_TILE, NB, BLK, BLK)
    rows_tiles = rows_comp.reshape(N_TILE, NB)
    cols_tiles = cols_comp.reshape(N_TILE, NB)

    def one_tile(packed):
        window_one, blocks_one, rows_one, cols_one = packed
        picked = jnp.take(window_one, cols_one, axis=1)
        product = jnp.einsum('brc,vbc->vbr', blocks_one.astype(jnp.float32), picked.astype(jnp.float32), precision=HIGHEST_PRECISION)
        onehot = (rows_one[None, :] == jnp.arange(RB, dtype=jnp.int32)[:, None]).astype(jnp.float32)
        summed = jnp.einsum('rb,vbi->vri', onehot, product, precision=HIGHEST_PRECISION)
        return summed.reshape(VAR, NODE, ELEM_DEV)

    result = lax.map(one_tile, (window, blocks, rows_tiles, cols_tiles))
    return jnp.moveaxis(result, 0, 2).reshape(VAR, NODE, N_TILE * ELEM_DEV)


def reference(state, metric, element_coupling, level_coupling, coeffs, edge_partner, sea_mask, forcing, remap_weights, remap_rows, remap_cols):
    states = []
    surfaces = []
    for component in range(2):
        state_out, surface = advance_component(state[component], metric[component], element_coupling[component], level_coupling[component], coeffs[component], edge_partner[component], sea_mask[component], forcing[component])
        states.append(state_out)
        surfaces.append(surface)
    forcings = []
    for component in range(2):
        forcings.append(remap(surfaces[1 - component], remap_weights[component], remap_rows[component], remap_cols[component]))
    return jnp.stack(states), jnp.stack(forcings)
```

```python
import functools

import jax
import jax.numpy as jnp
import numpy as np
from jax import lax
from jax.experimental import pallas as pl
from jax.experimental.pallas import tpu as pltpu
from jax.sharding import PartitionSpec as P

F32 = jnp.float32
BF16 = jnp.bfloat16
VMEM_LIMIT = 40 * 1024 * 1024


def dot(a, b):
    return jnp.dot(a, b, preferred_element_type=F32)


def iota(shape, dim):
    return lax.broadcasted_iota(jnp.int32, shape, dim)


def node_of(edge, place):
    side = jnp.where(edge == 1, 4 * place + 3, 4 * place)
    return jnp.where(edge == 0, place, jnp.where(edge == 3, 12 + place, side))


def split_rows(rows):
    group = rows // 64
    edge = jnp.where(group == 0, 0, jnp.where(group == 1, 3, group - 1))
    return edge, (rows % 64) // 4, rows % 4


def select_matrix():
    edge, level, place = split_rows(iota((256, 256), 0))
    wanted = level * 16 + node_of(edge, place)
    return (iota((256, 256), 1) == wanted).astype(BF16)


def spread_matrix():
    edge, level, place = split_rows(iota((256, 256), 1))
    wanted = level * 16 + node_of(edge, 3 - place)
    return (iota((256, 256), 0) == wanted).astype(BF16)


def coupling_matrices(node_ref, level_ref):
    row, col = iota((256, 16), 0), iota((256, 16), 1)
    rows_t, cols_t = iota((16, 256), 0), iota((16, 256), 1)
    inner, outer = (row % 16 == col).astype(BF16), (row // 16 == col).astype(BF16)
    inner_t, outer_t = (cols_t % 16 == rows_t).astype(BF16), (cols_t // 16 == rows_t).astype(BF16)
    r, c = iota((256, 256), 0), iota((256, 256), 1)
    node = dot(dot(inner, node_ref[0].astype(BF16)).astype(BF16), inner_t)
    node = jnp.where(r // 16 == c // 16, node, 0.0).astype(BF16)
    level = dot(dot(outer, level_ref[0].astype(BF16)).astype(BF16), outer_t)
    level = jnp.where(r % 16 == c % 16, level, 0.0).astype(BF16)
    return node, level


def diagonal(metric, penalty):
    node = iota((16, metric.shape[1]), 0)
    i, j = node // 4, node % 4
    edges = ((i == 0) | (i == 3)).astype(F32) + ((j == 0) | (j == 3)).astype(F32)
    return 0.8 - 0.3 * metric - penalty * edges


def exchange_rate(coeffs_ref, mask_ref):
    mask = mask_ref[0].astype(F32)
    return coeffs_ref[0, 1] * mask + coeffs_ref[0, 2] * (1.0 - mask)


def levels_of(pattern):
    return jnp.concatenate([pattern] * 16, axis=0)


def local_kernel(
    state_ref, metric_ref, node_ref, level_ref, coeffs_ref, partner_ref, mask_ref, forcing_ref,
    part_ref, even_ref, odd_ref, inner_ref, weights_ref, edges,
):
    penalty = coeffs_ref[0, 0]
    metric = metric_ref[...]
    node, level = coupling_matrices(node_ref, level_ref)
    weights_ref[:, 0:256] = node
    weights_ref[:, 256:512] = level
    weights_ref[:, 512:768] = spread_matrix()
    select = select_matrix()
    for step in range(4):
        columns = partner_ref[0:1, 512 + 256 * step : 768 + 256 * step] - 1024
        inner_ref[:, 256 * step : 256 * (step + 1)] = (iota((1024, 256), 0) == columns).astype(BF16)
    even = lax.rem(lax.axis_index("tile"), 2) == 0
    for v in range(4):
        rows = slice(256 * v, 256 * (v + 1))
        scaled = (penalty * state_ref[rows, :]).astype(BF16)
        picked = dot(select, scaled).astype(BF16)
        first, last = picked[0:64], picked[64:128]
        even_ref[64 * v : 64 * (v + 1), :] = jnp.where(even, last, first)
        odd_ref[64 * v : 64 * (v + 1), :] = jnp.where(even, first, last)
        edges[64 * v : 64 * (v + 1), 0:512] = picked[128:192]
        edges[64 * v : 64 * (v + 1), 512:1024] = picked[192:256]
    moved = dot(edges[...], inner_ref[...]).astype(BF16)
    factor = levels_of(diagonal(metric, penalty))
    rate = exchange_rate(coeffs_ref, mask_ref)
    for v in range(4):
        rows = slice(256 * v, 256 * (v + 1))
        u = state_ref[rows, :]
        near = moved[64 * v : 64 * (v + 1)]
        p = factor * u + dot(node, (u * metric).astype(BF16)) + dot(level, u.astype(BF16))
        p = p + dot(weights_ref[:, 640:704], near[:, 0:512]) + dot(weights_ref[:, 704:768], near[:, 512:1024])
        part_ref[rows, :] = p
        part_ref[256 * v : 256 * v + 16, :] += rate * (forcing_ref[0, v] - u[0:16])
        p = part_ref[rows, :]
        picked = dot(select[0:128], (penalty * p).astype(BF16)).astype(BF16)
        first, last = picked[0:64], picked[64:128]
        even_ref[256 + 64 * v : 320 + 64 * v, :] = jnp.where(even, last, first)
        odd_ref[256 + 64 * v : 320 + 64 * v, :] = jnp.where(even, first, last)


def tables_kernel(partner_ref, rows_ref, cols_ref, before_ref, after_ref, pick_ref, sum_ref):
    before_ref[...] = (iota((512, 512), 0) == partner_ref[0:1, 0:512]).astype(BF16)
    after_ref[...] = (iota((512, 512), 0) == partner_ref[0:1, 1536:2048] - 2560).astype(BF16)
    odd = lax.rem(lax.axis_index("tile"), 2)
    slots = rows_ref.shape[1]
    wide = 4 * slots
    repeat = (iota((slots, wide), 1) // 4 == iota((slots, wide), 0)).astype(BF16)
    widen = lambda ref: dot(jnp.broadcast_to(ref[0:1, :].astype(BF16), (16, slots)), repeat)[0:1].astype(jnp.int32)
    rows, cols = widen(rows_ref), widen(cols_ref)
    tile, block = cols // 64, cols % 64
    tile = jnp.where(odd == 1, 2 - tile, tile)
    var = iota((1, wide), 1) % 4
    wanted = tile * 256 + var * 64 + (block % 4) * 16 + block // 4
    pick_ref[...] = jnp.transpose((iota((768, wide), 0) == wanted).astype(F32)).astype(BF16)
    wanted = jnp.where(rows == 64, -1, var * 64 + (rows % 4) * 16 + rows // 4)
    sum_ref[...] = (iota((256, wide), 0) == wanted).astype(BF16)


def finish_kernel(
    state_ref, part_ref, even_ref, odd_ref, before_ref, after_ref, inner_ref, weights_ref,
    metric_ref, coeffs_ref, mask_ref, forcing_ref,
    next_ref, surface_ref, edges, halo_before, halo_after,
):
    penalty = coeffs_ref[0, 0]
    metric = metric_ref[...]
    even = lax.rem(lax.axis_index("tile"), 2) == 0
    halo_before[...] = dot(jnp.where(even, odd_ref[...], even_ref[...]), before_ref[...]).astype(BF16)
    halo_after[...] = dot(jnp.where(even, even_ref[...], odd_ref[...]), after_ref[...]).astype(BF16)
    select = select_matrix()
    spread = weights_ref[:, 512:768]
    for v in range(4):
        rows = slice(256 * v, 256 * (v + 1))
        quarter = slice(64 * v, 64 * (v + 1))
        u1 = part_ref[rows, :] + dot(spread[:, 0:64], halo_before[quarter]) + dot(spread[:, 64:128], halo_after[quarter])
        next_ref[rows, :] = u1
        picked = dot(select[128:256], (penalty * u1).astype(BF16)).astype(BF16)
        edges[quarter, 0:512] = picked[0:64]
        edges[quarter, 512:1024] = picked[64:128]
    moved = dot(edges[...], inner_ref[...]).astype(BF16)
    factor = levels_of(diagonal(metric, penalty))
    node = iota((256, 1), 0) % 16
    facing = jnp.where((node // 4 == 0) | (node // 4 == 3), penalty * penalty, 0.0)
    rate = exchange_rate(coeffs_ref, mask_ref)
    for v in range(4):
        rows = slice(256 * v, 256 * (v + 1))
        far = slice(256 + 64 * v, 256 + 64 * (v + 1))
        near = moved[64 * v : 64 * (v + 1)]
        u1 = next_ref[rows, :]
        x = factor * u1 + facing * state_ref[rows, :]
        x = x + dot(weights_ref[:, 0:256], (u1 * metric).astype(BF16)) + dot(weights_ref[:, 256:512], u1.astype(BF16))
        x = x + dot(spread[:, 0:64], halo_before[far]) + dot(spread[:, 64:128], halo_after[far])
        x = x + dot(spread[:, 128:192], near[:, 0:512]) + dot(spread[:, 192:256], near[:, 512:1024])
        next_ref[rows, :] = x
        lowest = x[0:16] + rate * (forcing_ref[0, v] - u1[0:16])
        next_ref[256 * v : 256 * v + 16, :] = lowest
        for q in range(4):
            surface_ref[64 * v + 16 * q : 64 * v + 16 * (q + 1), :] = lowest[:, 128 * q : 128 * (q + 1)].astype(BF16)


def remap_kernel(far_ref, own_ref, near_ref, pick_ref, sum_ref, blocks_ref, out_ref, products):
    picked = dot(pick_ref[:, 0:256], far_ref[...])
    picked = picked + dot(pick_ref[:, 256:512], own_ref[...])
    picked = picked + dot(pick_ref[:, 512:768], near_ref[...])
    slots = blocks_ref.shape[0]
    upper = iota((8, 1), 0) < 4
    for pair in range(slots // 2):
        part = picked[8 * pair : 8 * (pair + 1)]
        left = jnp.concatenate([jnp.where(upper, part, 0.0), jnp.where(upper, 0.0, part)], axis=1).astype(BF16)
        right = jnp.concatenate([blocks_ref[2 * pair], blocks_ref[2 * pair + 1]], axis=1)
        products[8 * pair : 8 * (pair + 1), :] = lax.dot_general(
            left, right, (((1,), (1,)), ((), ())), preferred_element_type=F32
        )
    value = products[...]
    high = value.astype(BF16)
    low = (value - high.astype(F32)).astype(BF16)
    total = dot(sum_ref[...], high) + dot(sum_ref[...], low)
    for v in range(4):
        for q in range(4):
            out_ref[0, v, :, 128 * q : 128 * (q + 1)] = total[64 * v + 16 * q : 64 * v + 16 * (q + 1)]


def call(kernel, outs, scratch=(), smem=(), count=0):
    vmem = pl.BlockSpec(memory_space=pltpu.VMEM)
    specs = [pl.BlockSpec(memory_space=pltpu.SMEM) if i in smem else vmem for i in range(count)]
    return pl.pallas_call(
        kernel,
        out_shape=[jax.ShapeDtypeStruct(shape, kind) for shape, kind in outs],
        in_specs=specs,
        out_specs=[vmem] * len(outs),
        scratch_shapes=list(scratch),
        compiler_params=pltpu.CompilerParams(vmem_limit_bytes=VMEM_LIMIT),
    )


def shards(
    state, metric, element_coupling, level_coupling, coeffs, edge_partner, sea_mask, forcing,
    remap_weights, remap_rows, remap_cols,
):
    tiles = lax.axis_size("tile")
    here = [(t, t ^ 1) for t in range(tiles)]
    away = [(t, (t + 1) % tiles if t % 2 else (t - 1) % tiles) for t in range(tiles)]
    crossed = lambda pairs: [(c * tiles + a, (1 - c) * tiles + b) for c in range(2) for a, b in pairs]
    straight = [(t, t) for t in range(tiles)]
    flat = state.reshape(1024, 512)
    part, even, odd, inner, weights = call(
        local_kernel,
        [((1024, 512), F32), ((512, 512), BF16), ((512, 512), BF16), ((1024, 1024), BF16), ((256, 768), BF16)],
        [pltpu.VMEM((256, 1024), BF16)], smem=(4,), count=8,
    )(flat, metric, element_coupling, level_coupling, coeffs, edge_partner, sea_mask, forcing)
    odd = lax.ppermute(odd, "tile", away)
    even = lax.ppermute(even, "tile", here)
    slots = remap_rows.shape[1]
    before, after, pick, total = call(
        tables_kernel,
        [((512, 512), BF16), ((512, 512), BF16), ((4 * slots, 768), BF16), ((256, 4 * slots), BF16)], count=3,
    )(edge_partner, remap_rows, remap_cols)
    nxt, surface = call(
        finish_kernel,
        [((1024, 512), F32), ((256, 128), BF16)],
        [pltpu.VMEM((256, 1024), BF16), pltpu.VMEM((512, 512), BF16), pltpu.VMEM((512, 512), BF16)],
        smem=(9,), count=12,
    )(flat, part, even, odd, before, after, inner, weights, metric, coeffs, sea_mask, forcing)
    far = lax.ppermute(surface, ("comp", "tile"), crossed(away))
    near = lax.ppermute(surface, ("comp", "tile"), crossed(here))
    own = lax.ppermute(surface, ("comp", "tile"), crossed(straight))
    (new_forcing,) = call(
        remap_kernel, [(forcing.shape, F32)], [pltpu.VMEM((4 * slots, 128), F32)], count=6,
    )(far, own, near, pick, total, remap_weights[0])
    return nxt.reshape(state.shape), new_forcing


def solution(mesh):
    placed = (
        P("comp", None, None, None, "tile"),
        P("comp", "tile"),
        P("comp", None, None),
        P("comp", None, None),
        P("comp", None),
        P("comp", "tile"),
        P("comp", None, "tile"),
        P("comp", None, None, "tile"),
        P("comp", "tile", None, None),
        P("comp", "tile"),
        P("comp", "tile"),
    )
    return jax.shard_map(
        shards,
        mesh=mesh,
        in_specs=placed,
        out_specs=(P("comp", None, None, None, "tile"), P("comp", None, None, "tile")),
        check_vma=False,
    )
```

```python
import functools

import jax
import jax.numpy as jnp
import numpy as np
from jax import lax
from jax.experimental import pallas as pl
from jax.experimental.pallas import tpu as pltpu
from jax.sharding import PartitionSpec as P

F32 = jnp.float32
BF16 = jnp.bfloat16
VMEM_LIMIT = 40 * 1024 * 1024


def dot(a, b):
    return jnp.dot(a, b, preferred_element_type=F32)


def iota(shape, dim):
    return lax.broadcasted_iota(jnp.int32, shape, dim)


def node_of(edge, place):
    side = jnp.where(edge == 1, 4 * place + 3, 4 * place)
    return jnp.where(edge == 0, place, jnp.where(edge == 3, 12 + place, side))


def split_rows(rows):
    group = rows // 64
    edge = jnp.where(group == 0, 0, jnp.where(group == 1, 3, group - 1))
    return edge, (rows % 64) // 4, rows % 4


def select_matrix():
    edge, level, place = split_rows(iota((256, 256), 0))
    wanted = level * 16 + node_of(edge, place)
    return (iota((256, 256), 1) == wanted).astype(BF16)


def spread_matrix():
    edge, level, place = split_rows(iota((256, 256), 1))
    wanted = level * 16 + node_of(edge, 3 - place)
    return (iota((256, 256), 0) == wanted).astype(BF16)


def coupling_matrices(node_ref, level_ref):
    row, col = iota((256, 16), 0), iota((256, 16), 1)
    rows_t, cols_t = iota((16, 256), 0), iota((16, 256), 1)
    inner, outer = (row % 16 == col).astype(BF16), (row // 16 == col).astype(BF16)
    inner_t, outer_t = (cols_t % 16 == rows_t).astype(BF16), (cols_t // 16 == rows_t).astype(BF16)
    r, c = iota((256, 256), 0), iota((256, 256), 1)
    node = dot(dot(inner, node_ref[0].astype(BF16)).astype(BF16), inner_t)
    node = jnp.where(r // 16 == c // 16, node, 0.0).astype(BF16)
    level = dot(dot(outer, level_ref[0].astype(BF16)).astype(BF16), outer_t)
    level = jnp.where(r % 16 == c % 16, level, 0.0).astype(BF16)
    return node, level


def diagonal(metric, penalty):
    node = iota((16, metric.shape[1]), 0)
    i, j = node // 4, node % 4
    edges = ((i == 0) | (i == 3)).astype(F32) + ((j == 0) | (j == 3)).astype(F32)
    return 0.8 - 0.3 * metric - penalty * edges


def exchange_rate(coeffs, mask):
    mask = mask.astype(F32)
    return coeffs[:, 1:2] * mask + coeffs[:, 2:3] * (1.0 - mask)


def levels_of(pattern):
    return jnp.concatenate([pattern] * 16, axis=0)


def halves(value):
    high = value.astype(BF16)
    return high, (value - high.astype(F32)).astype(BF16)


def low_select():
    row = iota((64, 64), 0)
    group = row // 16
    edge = jnp.where(group == 0, 0, jnp.where(group == 1, 3, group - 1))
    wanted = (row % 16 // 4) * 16 + node_of(edge, row % 4)
    return (iota((64, 64), 1) == wanted).astype(BF16)


def low_spread(first, second):
    col = iota((64, 64), 1)
    edge = jnp.where(col < 32, first, second)
    wanted = (col % 16 // 4) * 16 + node_of(edge, 3 - col % 4)
    return (iota((64, 64), 0) == wanted).astype(BF16)


def low_node_matrix(node):
    row, col = iota((64, 64), 0), iota((64, 64), 1)
    rows_of = (iota((64, 16), 0) % 16 == iota((64, 16), 1)).astype(BF16)
    cols_of = (iota((16, 64), 1) % 16 == iota((16, 64), 0)).astype(BF16)
    parts = [dot(dot(rows_of, part).astype(BF16), cols_of) for part in halves(node)]
    high, low = [jnp.where(row // 16 == col // 16, part, 0.0).astype(BF16) for part in parts]
    return jnp.concatenate([high, high, low], axis=1)


def low_node_product(matrix, value):
    high, low = halves(value)
    return dot(matrix, jnp.concatenate([high, low, high], axis=0))


def mix_to_lowest(level, ref, add):
    parts = []
    for v in range(4):
        total = add
        for m in range(16):
            term = level[0:1, m : m + 1] * ref[256 * v + 16 * m : 256 * v + 16 * (m + 1), :]
            total = term if total is None else total + term
        parts.append(total)
    return jnp.concatenate(parts, axis=0)


def local_kernel(
    state_hbm, metric_hbm, node_hbm, level_hbm, coeffs_hbm, partner_hbm, mask_hbm, forcing_hbm,
    part_ref, even_ref, odd_ref, even_low_ref, odd_low_ref, inner_ref, before_ref, after_ref,
    weights_ref, low_ref, base_ref, factor_ref, low_node_ref,
    state_ref, metric_ref, node_ref, level_ref, coeffs_ref, partner_ref, mask_ref, forcing_ref, edges, sems,
):
    copies = [
        pltpu.make_async_copy(source, target, sems.at[i])
        for i, (source, target) in enumerate([
            (partner_hbm, partner_ref), (node_hbm, node_ref), (level_hbm, level_ref), (coeffs_hbm, coeffs_ref),
            (metric_hbm, metric_ref), (state_hbm, state_ref), (mask_hbm, mask_ref), (forcing_hbm, forcing_ref),
        ])
    ]
    for copy in copies:
        copy.start()
    select, select_low = select_matrix(), low_select()
    spread_inner, spread = low_spread(1, 2), spread_matrix()
    weights_ref[:, 512:768] = spread
    for copy in copies[:5]:
        copy.wait()
    for step in range(4):
        columns = partner_ref[0:1, 512 + 256 * step : 768 + 256 * step] - 1024
        inner_ref[:, 256 * step : 256 * (step + 1)] = (iota((1024, 256), 0) == columns).astype(BF16)
    before_ref[...] = (iota((512, 512), 0) == partner_ref[0:1, 0:512]).astype(BF16)
    after_ref[...] = (iota((512, 512), 0) == partner_ref[0:1, 1536:2048] - 2560).astype(BF16)
    coeffs = coeffs_ref[...]
    penalty = coeffs[:, 0:1]
    metric = metric_ref[...]
    node, level = coupling_matrices(node_ref, level_ref)
    weights_ref[:, 0:256] = node
    weights_ref[:, 256:512] = level
    low_node = low_node_matrix(node_ref[0])
    low_node_ref[...] = low_node
    even = lax.rem(lax.axis_index("tile"), 2) == 0
    factor = diagonal(metric, penalty)
    for copy in copies[5:]:
        copy.wait()
    for v in range(4):
        scaled = (penalty * state_ref[256 * v : 256 * (v + 1), :]).astype(BF16)
        picked = dot(select, scaled).astype(BF16)
        first, last = picked[0:64], picked[64:128]
        even_ref[64 * v : 64 * (v + 1), :] = jnp.where(even, last, first)
        odd_ref[64 * v : 64 * (v + 1), :] = jnp.where(even, first, last)
        edges[64 * v : 64 * (v + 1), 0:512] = picked[128:192]
        edges[64 * v : 64 * (v + 1), 512:1024] = picked[192:256]
    lowest = jnp.concatenate([state_ref[256 * v : 256 * v + 16, :] for v in range(4)], axis=0)
    high, low = [dot(select_low, part).astype(BF16) for part in halves(penalty * lowest)]
    even_low_ref[0:16, :] = jnp.where(even, high[16:32], high[0:16])
    even_low_ref[16:32, :] = jnp.where(even, low[16:32], low[0:16])
    odd_low_ref[0:16, :] = jnp.where(even, high[0:16], high[16:32])
    odd_low_ref[16:32, :] = jnp.where(even, low[0:16], low[16:32])
    edges[256:272, 0:512] = high[32:48]
    edges[256:272, 512:1024] = high[48:64]
    edges[272:288, 0:512] = low[32:48]
    edges[272:288, 512:1024] = low[48:64]
    moved = dot(edges[...], inner_ref[...]).astype(BF16)
    rate = exchange_rate(coeffs, mask_ref[0])
    rates = jnp.concatenate([rate] * 4, axis=0)
    forced = rates * jnp.concatenate([forcing_ref[0, v] for v in range(4)], axis=0)
    factor_low = factor - rate
    factor_ref[...] = factor_low
    mixed = mix_to_lowest(level_ref[0], state_ref, None)
    near = moved[256:288]
    p_low = jnp.concatenate([factor_low] * 4, axis=0) * lowest + forced + mixed
    p_low = p_low + low_node_product(low_node, lowest * metric)
    p_low = p_low + dot(spread_inner, jnp.concatenate([near[:, 0:512], near[:, 512:1024]], axis=0))
    low_ref[...] = p_low
    high, low = [dot(select_low[0:32], part).astype(BF16) for part in halves(penalty * (p_low + mixed))]
    even_low_ref[32:48, :] = jnp.where(even, high[16:32], high[0:16])
    even_low_ref[48:64, :] = jnp.where(even, low[16:32], low[0:16])
    odd_low_ref[32:48, :] = jnp.where(even, high[0:16], high[16:32])
    odd_low_ref[48:64, :] = jnp.where(even, low[0:16], low[16:32])
    factors = levels_of(factor)
    for v in range(4):
        rows = slice(256 * v, 256 * (v + 1))
        u = state_ref[rows, :]
        near = moved[64 * v : 64 * (v + 1)]
        p = factors * u + dot(node, (u * metric).astype(BF16)) + dot(level, u.astype(BF16))
        p = p + dot(spread[:, 128:192], near[:, 0:512]) + dot(spread[:, 192:256], near[:, 512:1024])
        p = jnp.concatenate([p_low[16 * v : 16 * (v + 1)], p[16:256]], axis=0)
        part_ref[rows, :] = p
        picked = dot(select[0:128], (penalty * p).astype(BF16)).astype(BF16)
        first, last = picked[0:64], picked[64:128]
        even_ref[256 + 64 * v : 320 + 64 * v, :] = jnp.where(even, last, first)
        odd_ref[256 + 64 * v : 320 + 64 * v, :] = jnp.where(even, first, last)
    mixed = mix_to_lowest(level_ref[0], part_ref, None)
    node_at = iota((64, 1), 0) % 16
    facing = jnp.where((node_at // 4 == 0) | (node_at // 4 == 3), penalty * penalty, 0.0)
    base_ref[...] = mixed + forced + facing * lowest


def lowest_kernel(
    low_ref, base_ref, factor_ref, low_node_ref, metric_ref, coeffs_ref, even_ref, odd_ref, before_ref, after_ref, inner_ref,
    surface_ref,
):
    penalty = coeffs_ref[:, 0:1]
    even = lax.rem(lax.axis_index("tile"), 2) == 0
    before = dot(jnp.where(even, odd_ref[...], even_ref[...]), before_ref[...]).astype(BF16)
    after = dot(jnp.where(even, even_ref[...], odd_ref[...]), after_ref[...]).astype(BF16)
    outer, inner, select = low_spread(0, 3), low_spread(1, 2), low_select()
    u1 = low_ref[...] + dot(outer, jnp.concatenate([before[0:32], after[0:32]], axis=0))
    high, low = [dot(select[32:64], part).astype(BF16) for part in halves(penalty * u1)]
    sides = [jnp.concatenate([high[at : at + 16], low[at : at + 16]], axis=0) for at in (0, 16)]
    near = dot(jnp.concatenate(sides, axis=1), inner_ref[...]).astype(BF16)
    x = base_ref[...] + jnp.concatenate([factor_ref[...]] * 4, axis=0) * u1
    x = x + low_node_product(low_node_ref[...], u1 * metric_ref[...])
    x = x + dot(outer, jnp.concatenate([before[32:64], after[32:64]], axis=0))
    x = x + dot(inner, jnp.concatenate([near[:, 0:512], near[:, 512:1024]], axis=0))
    x = x.astype(BF16)
    for v in range(4):
        for q in range(4):
            surface_ref[64 * v + 16 * q : 64 * v + 16 * (q + 1), :] = x[16 * v : 16 * (v + 1), 128 * q : 128 * (q + 1)]


def tables_kernel(rows_ref, cols_ref, even_in, odd_in, pick_ref, sum_ref, even_out, odd_out):
    odd = lax.rem(lax.axis_index("tile"), 2)
    slots = rows_ref.shape[1]
    wide = 4 * slots
    repeat = (iota((slots, wide), 1) // 4 == iota((slots, wide), 0)).astype(BF16)
    widen = lambda ref: dot(jnp.broadcast_to(ref[0:1, :].astype(BF16), (16, slots)), repeat)[0:1].astype(jnp.int32)
    rows, cols = widen(rows_ref), widen(cols_ref)
    tile, block = cols // 64, cols % 64
    tile = jnp.where(odd == 1, 2 - tile, tile)
    var = iota((1, wide), 1) % 4
    wanted = tile * 256 + var * 64 + (block % 4) * 16 + block // 4
    pick_ref[...] = jnp.transpose((iota((768, wide), 0) == wanted).astype(F32)).astype(BF16)
    wanted = jnp.where(rows == 64, -1, var * 64 + (rows % 4) * 16 + rows // 4)
    sum_ref[...] = (iota((256, wide), 0) == wanted).astype(BF16)


def finish_kernel(
    state_ref, part_ref, even_ref, odd_ref, before_ref, after_ref, inner_ref, weights_ref,
    metric_ref, coeffs_ref, mask_ref, forcing_ref,
    next_hbm, next_ref, edges, halo_before, halo_after, sems,
):
    coeffs = coeffs_ref[...]
    penalty = coeffs[:, 0:1]
    metric = metric_ref[...]
    even = lax.rem(lax.axis_index("tile"), 2) == 0
    halo_before[...] = dot(jnp.where(even, odd_ref[...], even_ref[...]), before_ref[...]).astype(BF16)
    halo_after[...] = dot(jnp.where(even, even_ref[...], odd_ref[...]), after_ref[...]).astype(BF16)
    select = select_matrix()
    spread = weights_ref[:, 512:768]
    for v in range(4):
        rows = slice(256 * v, 256 * (v + 1))
        quarter = slice(64 * v, 64 * (v + 1))
        u1 = part_ref[rows, :] + dot(spread[:, 0:64], halo_before[quarter]) + dot(spread[:, 64:128], halo_after[quarter])
        next_ref[rows, :] = u1
        picked = dot(select[128:256], (penalty * u1).astype(BF16)).astype(BF16)
        edges[quarter, 0:512] = picked[0:64]
        edges[quarter, 512:1024] = picked[64:128]
    moved = dot(edges[...], inner_ref[...]).astype(BF16)
    factor = levels_of(diagonal(metric, penalty))
    node = iota((256, 1), 0) % 16
    facing = jnp.where((node // 4 == 0) | (node // 4 == 3), penalty * penalty, 0.0)
    rate = exchange_rate(coeffs, mask_ref[0])
    copies = []
    for v in range(4):
        rows = slice(256 * v, 256 * (v + 1))
        far = slice(256 + 64 * v, 256 + 64 * (v + 1))
        near = moved[64 * v : 64 * (v + 1)]
        u1 = next_ref[rows, :]
        x = factor * u1 + facing * state_ref[rows, :]
        x = x + dot(weights_ref[:, 0:256], (u1 * metric).astype(BF16)) + dot(weights_ref[:, 256:512], u1.astype(BF16))
        x = x + dot(spread[:, 0:64], halo_before[far]) + dot(spread[:, 64:128], halo_after[far])
        x = x + dot(spread[:, 128:192], near[:, 0:512]) + dot(spread[:, 192:256], near[:, 512:1024])
        next_ref[rows, :] = x
        lowest = x[0:16] + rate * (forcing_ref[0, v] - u1[0:16])
        next_ref[256 * v : 256 * v + 16, :] = lowest
        copies.append(pltpu.make_async_copy(next_ref.at[rows], next_hbm.at[rows], sems.at[v]))
        copies[-1].start()
    for copy in copies:
        copy.wait()


def remap_kernel(own_ref, near_ref, far_ref, pick_ref, sum_ref, blocks_ref, out_ref, products):
    picked = dot(pick_ref[:, 0:256], far_ref[...])
    picked = picked + dot(pick_ref[:, 256:512], own_ref[...])
    picked = picked + dot(pick_ref[:, 512:768], near_ref[...])
    slots = blocks_ref.shape[0]
    upper = iota((8, 1), 0) < 4
    for pair in range(slots // 2):
        part = picked[8 * pair : 8 * (pair + 1)]
        left = jnp.concatenate([jnp.where(upper, part, 0.0), jnp.where(upper, 0.0, part)], axis=1).astype(BF16)
        right = jnp.concatenate([blocks_ref[2 * pair], blocks_ref[2 * pair + 1]], axis=1)
        products[8 * pair : 8 * (pair + 1), :] = lax.dot_general(
            left, right, (((1,), (1,)), ((), ())), preferred_element_type=F32
        )
    value = products[...]
    high = value.astype(BF16)
    low = (value - high.astype(F32)).astype(BF16)
    total = dot(sum_ref[...], high) + dot(sum_ref[...], low)
    for v in range(4):
        for q in range(4):
            out_ref[0, v, :, 128 * q : 128 * (q + 1)] = total[64 * v + 16 * q : 64 * v + 16 * (q + 1)]


def call(kernel, outs, scratch=(), inputs="", results="", aliases={}, cost=0):
    spaces = {"v": pltpu.VMEM, "h": pltpu.HBM, "a": pl.ANY}
    place = lambda kind: pl.BlockSpec(memory_space=spaces[kind])
    results = results or "v" * len(outs)
    return pl.pallas_call(
        kernel,
        out_shape=[jax.ShapeDtypeStruct(shape, kind) for shape, kind in outs],
        in_specs=[place(kind) for kind in inputs],
        out_specs=[place(kind) for kind in results],
        input_output_aliases=aliases,
        scratch_shapes=list(scratch),
        cost_estimate=pl.CostEstimate(flops=cost, bytes_accessed=0, transcendentals=0) if cost else None,
        compiler_params=pltpu.CompilerParams(vmem_limit_bytes=VMEM_LIMIT),
    )


def shards(
    state, metric, element_coupling, level_coupling, coeffs, edge_partner, sea_mask, forcing,
    remap_weights, remap_rows, remap_cols,
):
    tiles = lax.axis_size("tile")
    here = [(t, t ^ 1) for t in range(tiles)]
    away = [(t, (t + 1) % tiles if t % 2 else (t - 1) % tiles) for t in range(tiles)]
    crossed = lambda pairs: [(c * tiles + a, (1 - c) * tiles + b) for c in range(2) for a, b in pairs]
    straight = [(t, t) for t in range(tiles)]
    flat = state.reshape(1024, 512)
    inputs = (flat, metric, element_coupling, level_coupling, coeffs, edge_partner, sea_mask, forcing)
    (part, even, odd, even_low, odd_low, inner, before, after, weights, low, base, factor, low_node) = call(
        local_kernel,
        [
            ((1024, 512), F32), ((512, 512), BF16), ((512, 512), BF16), ((64, 512), BF16), ((64, 512), BF16),
            ((1024, 1024), BF16), ((512, 512), BF16), ((512, 512), BF16), ((256, 768), BF16),
            ((64, 512), F32), ((64, 512), F32), ((16, 512), F32), ((64, 192), BF16),
        ],
        [pltpu.VMEM(value.shape, value.dtype) for value in inputs]
        + [pltpu.VMEM((288, 1024), BF16), pltpu.SemaphoreType.DMA((8,))],
        "hhhhhhhh",
    )(*[pltpu.with_memory_space_constraint(value, pltpu.HBM) for value in inputs])
    odd_low = lax.ppermute(odd_low, "tile", away)
    even_low = lax.ppermute(even_low, "tile", here)
    slots = remap_rows.shape[1]
    pick, total, even, odd = call(
        tables_kernel,
        [((4 * slots, 768), BF16), ((256, 4 * slots), BF16), (even.shape, BF16), (odd.shape, BF16)],
        inputs="vvaa", results="vvaa", aliases={2: 2, 3: 3}, cost=4_000_000_000,
    )(remap_rows, remap_cols, even, odd)
    odd = lax.ppermute(odd, "tile", away)
    even = lax.ppermute(even, "tile", here)
    (surface,) = call(lowest_kernel, [((256, 128), BF16)], inputs="v" * 11, cost=40_000_000_000)(
        low, base, factor, low_node, metric, coeffs, even_low, odd_low, before, after, inner
    )
    far = lax.ppermute(surface, ("comp", "tile"), crossed(away))
    near = lax.ppermute(surface, ("comp", "tile"), crossed(here))
    own = lax.ppermute(surface, ("comp", "tile"), crossed(straight))
    (nxt,) = call(
        finish_kernel,
        [((1024, 512), F32)],
        [
            pltpu.VMEM((1024, 512), F32), pltpu.VMEM((256, 1024), BF16), pltpu.VMEM((512, 512), BF16),
            pltpu.VMEM((512, 512), BF16), pltpu.SemaphoreType.DMA((4,)),
        ],
        "v" * 12, "h",
    )(flat, part, even, odd, before, after, inner, weights, metric, coeffs, sea_mask, forcing)
    (new_forcing,) = call(
        remap_kernel, [(forcing.shape, F32)], [pltpu.VMEM((4 * slots, 128), F32)], "v" * 6,
    )(own, near, far, pick, total, remap_weights[0])
    return nxt.reshape(state.shape), new_forcing


def solution(mesh):
    placed = (
        P("comp", None, None, None, "tile"),
        P("comp", "tile"),
        P("comp", None, None),
        P("comp", None, None),
        P("comp", None),
        P("comp", "tile"),
        P("comp", None, "tile"),
        P("comp", None, None, "tile"),
        P("comp", "tile", None, None),
        P("comp", "tile"),
        P("comp", "tile"),
    )
    return jax.shard_map(
        shards,
        mesh=mesh,
        in_specs=placed,
        out_specs=(P("comp", None, None, None, "tile"), P("comp", None, None, "tile")),
        check_vma=False,
    )
```

```python
import functools

import jax
import jax.numpy as jnp
import numpy as np
from jax import lax
from jax.experimental import pallas as pl
from jax.experimental.pallas import tpu as pltpu
from jax.sharding import PartitionSpec as P

F32 = jnp.float32
BF16 = jnp.bfloat16
VMEM_LIMIT = 40 * 1024 * 1024


def dot(a, b):
    return jnp.dot(a, b, preferred_element_type=F32)


def iota(shape, dim):
    return lax.broadcasted_iota(jnp.int32, shape, dim)


def ends():
    here = jnp.where(lax.rem(lax.axis_index("tile"), 2) == 0, 12, 0)
    return here, 12 - here


def group_node(group, place):
    here, away = ends()
    side = jnp.where(group == 2, 4 * place + 3, 4 * place)
    return jnp.where(group == 0, here + place, jnp.where(group == 1, away + place, side))


def spread_matrix():
    col = iota((256, 256), 1)
    wanted = (col % 16) * 16 + group_node(col // 64, 3 - col // 16 % 4)
    return (iota((256, 256), 0) == wanted).astype(BF16)


def coupling_matrices(node_ref, level_ref):
    rows, cols = iota((16, 256), 0), iota((16, 256), 1)
    inner, outer = (cols % 16 == rows).astype(BF16), (cols // 16 == rows).astype(BF16)
    r, c = iota((256, 256), 0), iota((256, 256), 1)
    node = jnp.concatenate([dot(node_ref[0].astype(BF16), inner)] * 16, axis=0)
    node = jnp.where(r // 16 == c // 16, node, 0.0).astype(BF16)
    level = dot(level_ref[0].astype(BF16), outer)
    level = jnp.concatenate([jnp.broadcast_to(level[l : l + 1], (16, 256)) for l in range(16)], axis=0)
    level = jnp.where(r % 16 == c % 16, level, 0.0).astype(BF16)
    return node, level


def diagonal(metric, penalty):
    node = iota((16, metric.shape[1]), 0)
    i, j = node // 4, node % 4
    edges = ((i == 0) | (i == 3)).astype(F32) + ((j == 0) | (j == 3)).astype(F32)
    return 0.8 - 0.3 * metric - penalty * edges


def exchange_rate(coeffs_ref, mask):
    mask = mask.astype(F32)
    return coeffs_ref[0, 1] * mask + coeffs_ref[0, 2] * (1.0 - mask)


def levels_of(pattern):
    return jnp.concatenate([pattern] * 16, axis=0)


def halves(value):
    high = value.astype(BF16)
    return high, (value - high.astype(F32)).astype(BF16)


def low_select():
    row = iota((64, 64), 0)
    wanted = (row % 16 // 4) * 16 + group_node(row // 16, row % 4)
    return (iota((64, 64), 1) == wanted).astype(BF16)


def low_spread(first, second):
    col = iota((64, 64), 1)
    wanted = (col % 16 // 4) * 16 + group_node(jnp.where(col < 32, first, second), 3 - col % 4)
    return (iota((64, 64), 0) == wanted).astype(BF16)


def low_node_matrix(node):
    row, col = iota((64, 64), 0), iota((64, 64), 1)
    rows_of = (iota((64, 16), 0) % 16 == iota((64, 16), 1)).astype(BF16)
    cols_of = (iota((16, 64), 1) % 16 == iota((16, 64), 0)).astype(BF16)
    parts = [dot(dot(rows_of, part).astype(BF16), cols_of) for part in halves(node)]
    high, low = [jnp.where(row // 16 == col // 16, part, 0.0).astype(BF16) for part in parts]
    return jnp.concatenate([high, high, low], axis=1)


def low_node_product(matrix, value):
    high, low = halves(value)
    return dot(matrix, jnp.concatenate([high, low, high], axis=0))


LANES = [slice(128 * c, 128 * (c + 1)) for c in range(4)]
SIDE_NODES = ((3, 7, 11, 15), (0, 4, 8, 12))


def whole_rows(ref, start, count):
    return jnp.concatenate([ref[c, start : start + count, :] for c in range(4)], axis=1)


def mix_to_lowest(level, ref):
    parts = []
    for v in range(4):
        total = level[0, 0, 0] * whole_rows(ref, 256 * v, 16)
        for m in range(1, 16):
            total = total + level[0, 0, m] * whole_rows(ref, 256 * v + 16 * m, 16)
        parts.append(total)
    return jnp.concatenate(parts, axis=0)


def pack_node(ref, v, c, node, scale):
    return (scale * ref[c, pl.ds(256 * v + node, 16, stride=16), :]).astype(BF16)


def pack_facing(ref, scale, here_ref, away_ref, start):
    for target, first in zip((here_ref, away_ref), ends()):
        for v in range(4):
            for place in range(4):
                at = start + 64 * v + 16 * place
                for c in range(4):
                    target[at : at + 16, LANES[c]] = pack_node(ref, v, c, first + place, scale)


def pack_sides(ref, scale, edges):
    for side in range(2):
        for v in range(4):
            for place in range(4):
                at = 64 * v + 16 * place
                for c in range(4):
                    lanes = slice(512 * side + 128 * c, 512 * side + 128 * (c + 1))
                    edges[at : at + 16, lanes] = pack_node(ref, v, c, SIDE_NODES[side][place], scale)


def local_kernel(
    state_hbm, metric_hbm, node_hbm, level_hbm, coeffs_hbm, partner_hbm, mask_hbm, forcing_hbm,
    state_ref, part_ref, here_ref, away_ref, here_low_ref, away_low_ref, inner_ref,
    weights_ref, low_ref, base_ref, factor_ref, low_node_ref,
    metric_ref, node_ref, level_ref, coeffs_ref, partner_ref, mask_ref, forcing_ref, level_smem, edges, sems,
):
    pairs = [
        (partner_hbm, partner_ref), (node_hbm, node_ref), (level_hbm, level_ref), (coeffs_hbm, coeffs_ref),
        (metric_hbm, metric_ref),
    ]
    pairs += [(state_hbm.at[:, LANES[c]], state_ref.at[c]) for c in range(4)]
    pairs += [(mask_hbm, mask_ref), (forcing_hbm, forcing_ref), (level_hbm, level_smem)]
    copies = [pltpu.make_async_copy(source, target, sems.at[i]) for i, (source, target) in enumerate(pairs)]
    for copy in copies:
        copy.start()
    select_low, spread_inner = low_select(), low_spread(2, 3)
    weights_ref[:, 512:768] = spread_matrix()
    for copy in copies[:5]:
        copy.wait()
    for step in range(4):
        columns = partner_ref[0:1, 512 + 256 * step : 768 + 256 * step] - 1024
        hit = iota((1024, 256), 0) == columns
        inner_ref[:, 256 * step : 256 * (step + 1)] = jnp.where(hit, 1.0, 0.0).astype(BF16)
    penalty = coeffs_ref[0, 0]
    metric = metric_ref[...]
    node, level = coupling_matrices(node_ref, level_ref)
    weights_ref[:, 0:256] = node
    weights_ref[:, 256:512] = level
    low_node = low_node_matrix(node_ref[0])
    low_node_ref[...] = low_node
    factor = diagonal(metric, penalty)
    for copy in copies[5:]:
        copy.wait()
    pack_sides(state_ref, penalty, edges)
    lowest = jnp.concatenate([whole_rows(state_ref, 256 * v, 16) for v in range(4)], axis=0)
    high, low = [dot(select_low, part).astype(BF16) for part in halves(penalty * lowest)]
    here_low_ref[0:16, :] = high[0:16]
    here_low_ref[16:32, :] = low[0:16]
    away_low_ref[0:16, :] = high[16:32]
    away_low_ref[16:32, :] = low[16:32]
    edges[256:272, 0:512] = high[32:48]
    edges[256:272, 512:1024] = high[48:64]
    edges[272:288, 0:512] = low[32:48]
    edges[272:288, 512:1024] = low[48:64]
    moved = dot(edges[...], inner_ref[...]).astype(BF16)
    pack_facing(state_ref, penalty, here_ref, away_ref, 0)
    rate = exchange_rate(coeffs_ref, mask_ref[0])
    rates = jnp.concatenate([rate] * 4, axis=0)
    forced = rates * jnp.concatenate([forcing_ref[0, v] for v in range(4)], axis=0)
    factor_low = factor - rate
    factor_ref[...] = factor_low
    mixed = mix_to_lowest(level_smem, state_ref)
    near = moved[256:288]
    p_low = jnp.concatenate([factor_low] * 4, axis=0) * lowest + forced + mixed
    p_low = p_low + low_node_product(low_node, lowest * metric)
    p_low = p_low + dot(spread_inner, jnp.concatenate([near[:, 0:512], near[:, 512:1024]], axis=0))
    low_ref[...] = p_low
    high, low = [dot(select_low[0:32], part).astype(BF16) for part in halves(penalty * (p_low + mixed))]
    here_low_ref[32:48, :] = high[0:16]
    here_low_ref[48:64, :] = low[0:16]
    away_low_ref[32:48, :] = high[16:32]
    away_low_ref[48:64, :] = low[16:32]
    factors = levels_of(factor)
    for v in range(4):
        u = whole_rows(state_ref, 256 * v, 256)
        operand = [(u * metric).astype(BF16), u.astype(BF16)]
        operand += [moved[64 * v : 64 * (v + 1), 512 * side : 512 * (side + 1)] for side in range(2)]
        p = dot(jnp.concatenate([weights_ref[:, 0:512], weights_ref[:, 640:768]], axis=1), jnp.concatenate(operand, axis=0))
        p = jnp.concatenate([p_low[16 * v : 16 * (v + 1)], (factors * u + p)[16:256]], axis=0)
        for c in range(4):
            part_ref[c, 256 * v : 256 * (v + 1), :] = p[:, LANES[c]]
    pack_facing(part_ref, penalty, here_ref, away_ref, 256)
    mixed = mix_to_lowest(level_smem, part_ref)
    node_at = iota((64, 1), 0) % 16
    facing = jnp.where((node_at // 4 == 0) | (node_at // 4 == 3), penalty * penalty, 0.0)
    base_ref[...] = mixed + forced + facing * lowest


def lowest_kernel(
    low_ref, base_ref, factor_ref, low_node_ref, metric_ref, coeffs_ref, here_ref, away_ref, here_map, away_map, inner_ref,
    surface_ref,
):
    penalty = coeffs_ref[:, 0:1]
    here = dot(here_ref[...], here_map[...]).astype(BF16)
    away = dot(away_ref[...], away_map[...]).astype(BF16)
    outer, inner, select = low_spread(0, 1), low_spread(2, 3), low_select()
    u1 = low_ref[...] + dot(outer, jnp.concatenate([here[0:32], away[0:32]], axis=0))
    high, low = [dot(select[32:64], part).astype(BF16) for part in halves(penalty * u1)]
    sides = [jnp.concatenate([high[at : at + 16], low[at : at + 16]], axis=0) for at in (0, 16)]
    near = dot(jnp.concatenate(sides, axis=1), inner_ref[...]).astype(BF16)
    x = base_ref[...] + jnp.concatenate([factor_ref[...]] * 4, axis=0) * u1
    x = x + low_node_product(low_node_ref[...], u1 * metric_ref[...])
    x = x + dot(outer, jnp.concatenate([here[32:64], away[32:64]], axis=0))
    x = x + dot(inner, jnp.concatenate([near[:, 0:512], near[:, 512:1024]], axis=0))
    x = x.astype(BF16)
    for v in range(4):
        for q in range(4):
            surface_ref[64 * v + 16 * q : 64 * v + 16 * (q + 1), :] = x[16 * v : 16 * (v + 1), 128 * q : 128 * (q + 1)]


def tables_kernel(
    partner_ref, rows_ref, cols_ref, here_in, away_in,
    here_map, away_map, pick_ref, sum_ref, here_out, away_out,
):
    last = ends()[0] == 12
    before, after = partner_ref[0:1, 0:512], partner_ref[0:1, 1536:2048] - 2560
    here_map[...] = jnp.where(iota((512, 512), 0) == jnp.where(last, after, before), 1.0, 0.0).astype(BF16)
    away_map[...] = jnp.where(iota((512, 512), 0) == jnp.where(last, before, after), 1.0, 0.0).astype(BF16)
    odd = lax.rem(lax.axis_index("tile"), 2)
    slots = rows_ref.shape[1]
    wide = 4 * slots
    repeat = (iota((slots, wide), 1) // 4 == iota((slots, wide), 0)).astype(BF16)
    widen = lambda ref: dot(jnp.broadcast_to(ref[0:1, :].astype(BF16), (16, slots)), repeat)[0:1].astype(jnp.int32)
    rows, cols = widen(rows_ref), widen(cols_ref)
    tile, block = cols // 64, cols % 64
    tile = jnp.where(odd == 1, 2 - tile, tile)
    var = iota((1, wide), 1) % 4
    wanted = tile * 256 + var * 64 + (block % 4) * 16 + block // 4
    pick_ref[...] = jnp.transpose((iota((768, wide), 0) == wanted).astype(F32)).astype(BF16)
    wanted = jnp.where(rows == 64, -1, var * 64 + (rows % 4) * 16 + rows // 4)
    sum_ref[...] = (iota((256, wide), 0) == wanted).astype(BF16)


def finish_kernel(
    state_ref, part_ref, here_ref, away_ref, here_map, away_map, inner_ref, weights_ref,
    metric_ref, coeffs_ref, mask_ref, forcing_ref,
    next_hbm, middle_ref, next_ref, edges, sems,
):
    penalty = coeffs_ref[:, 0:1]
    metric = metric_ref[...]
    here = dot(here_ref[...], here_map[...]).astype(BF16)
    away = dot(away_ref[...], away_map[...]).astype(BF16)
    for v in range(4):
        rows = slice(64 * v, 64 * (v + 1))
        halo = dot(weights_ref[:, 512:640], jnp.concatenate([here[rows], away[rows]], axis=0))
        for c in range(4):
            middle_ref[c, 256 * v : 256 * (v + 1), :] = part_ref[c, 256 * v : 256 * (v + 1), :] + halo[:, LANES[c]]
    pack_sides(middle_ref, penalty, edges)
    moved = dot(edges[...], inner_ref[...]).astype(BF16)
    factors = levels_of(diagonal(metric, penalty))
    node = iota((256, 1), 0) % 16
    facing = jnp.where((node // 4 == 0) | (node // 4 == 3), penalty * penalty, 0.0)
    mask = mask_ref[0].astype(F32)
    rate = coeffs_ref[:, 1:2] * mask + coeffs_ref[:, 2:3] * (1.0 - mask)
    copies = []
    for v in range(4):
        u1 = whole_rows(middle_ref, 256 * v, 256)
        rows = slice(64 * v, 64 * (v + 1))
        far = slice(256 + 64 * v, 256 + 64 * (v + 1))
        operand = [(u1 * metric).astype(BF16), u1.astype(BF16), here[far], away[far]]
        operand += [moved[rows, 512 * side : 512 * (side + 1)] for side in range(2)]
        x = factors * u1 + facing * whole_rows(state_ref, 256 * v, 256)
        x = x + dot(weights_ref[...], jnp.concatenate(operand, axis=0))
        added = rate * (forcing_ref[0, v] - u1[0:16])
        next_ref[256 * v : 256 * (v + 1), :] = jnp.concatenate([x[0:16] + added, x[16:256]], axis=0)
        rows = pl.ds(256 * v, 256)
        copies.append(pltpu.make_async_copy(next_ref.at[rows], next_hbm.at[rows], sems.at[v]))
        copies[-1].start()
    for copy in copies:
        copy.wait()


def remap_kernel(own_ref, near_ref, far_ref, pick_ref, sum_ref, blocks_ref, out_ref, products):
    picked = dot(pick_ref[:, 0:256], far_ref[...])
    picked = picked + dot(pick_ref[:, 256:512], own_ref[...])
    picked = picked + dot(pick_ref[:, 512:768], near_ref[...])
    slots = blocks_ref.shape[0]
    upper = iota((8, 1), 0) < 4
    for pair in range(slots // 2):
        part = picked[8 * pair : 8 * (pair + 1)]
        left = jnp.concatenate([jnp.where(upper, part, 0.0), jnp.where(upper, 0.0, part)], axis=1).astype(BF16)
        right = jnp.concatenate([blocks_ref[2 * pair], blocks_ref[2 * pair + 1]], axis=1)
        products[8 * pair : 8 * (pair + 1), :] = lax.dot_general(
            left, right, (((1,), (1,)), ((), ())), preferred_element_type=F32
        )
    value = products[...]
    high = value.astype(BF16)
    low = (value - high.astype(F32)).astype(BF16)
    total = dot(sum_ref[...], high) + dot(sum_ref[...], low)
    for v in range(4):
        for q in range(4):
            out_ref[0, v, :, 128 * q : 128 * (q + 1)] = total[64 * v + 16 * q : 64 * v + 16 * (q + 1)]


def call(kernel, outs, scratch=(), inputs="", results="", aliases={}, cost=0):
    spaces = {"v": pltpu.VMEM, "s": pltpu.SMEM, "h": pltpu.HBM, "a": pl.ANY}
    place = lambda kind: pl.BlockSpec(memory_space=spaces[kind])
    results = results or "v" * len(outs)
    return pl.pallas_call(
        kernel,
        out_shape=[jax.ShapeDtypeStruct(shape, kind) for shape, kind in outs],
        in_specs=[place(kind) for kind in inputs],
        out_specs=[place(kind) for kind in results],
        input_output_aliases=aliases,
        scratch_shapes=list(scratch),
        cost_estimate=pl.CostEstimate(flops=cost, bytes_accessed=0, transcendentals=0) if cost else None,
        compiler_params=pltpu.CompilerParams(vmem_limit_bytes=VMEM_LIMIT),
    )


def shards(
    state, metric, element_coupling, level_coupling, coeffs, edge_partner, sea_mask, forcing,
    remap_weights, remap_rows, remap_cols,
):
    tiles = lax.axis_size("tile")
    here = [(t, t ^ 1) for t in range(tiles)]
    away = [(t, (t + 1) % tiles if t % 2 else (t - 1) % tiles) for t in range(tiles)]
    crossed = lambda pairs: [(c * tiles + a, (1 - c) * tiles + b) for c in range(2) for a, b in pairs]
    straight = [(t, t) for t in range(tiles)]
    flat = state.reshape(1024, 512)
    inputs = (flat, metric, element_coupling, level_coupling, coeffs, edge_partner, sea_mask, forcing)
    (chunks, part, here_edge, away_edge, here_low, away_low, inner, weights, low, base, factor, low_node) = call(
        local_kernel,
        [
            ((4, 1024, 128), F32), ((4, 1024, 128), F32), ((512, 512), BF16), ((512, 512), BF16), ((64, 512), BF16),
            ((64, 512), BF16), ((1024, 1024), BF16), ((256, 768), BF16),
            ((64, 512), F32), ((64, 512), F32), ((16, 512), F32), ((64, 192), BF16),
        ],
        [(pltpu.SMEM if value is coeffs else pltpu.VMEM)(value.shape, value.dtype) for value in inputs[1:]]
        + [pltpu.SMEM((1, 16, 16), F32), pltpu.VMEM((288, 1024), BF16), pltpu.SemaphoreType.DMA((12,))],
        "hhhhhhhh",
    )(*[pltpu.with_memory_space_constraint(value, pltpu.HBM) for value in inputs])
    away_low = lax.ppermute(away_low, "tile", away)
    here_low = lax.ppermute(here_low, "tile", here)
    slots = remap_rows.shape[1]
    here_map, away_map, pick, total, here_edge, away_edge = call(
        tables_kernel,
        [
            ((512, 512), BF16), ((512, 512), BF16), ((4 * slots, 768), BF16), ((256, 4 * slots), BF16),
            (here_edge.shape, BF16), (away_edge.shape, BF16),
        ],
        inputs="vvvaa", results="vvvvaa", aliases={3: 4, 4: 5}, cost=4_000_000_000,
    )(edge_partner, remap_rows, remap_cols, here_edge, away_edge)
    away_edge = lax.ppermute(away_edge, "tile", away)
    here_edge = lax.ppermute(here_edge, "tile", here)
    (surface,) = call(lowest_kernel, [((256, 128), BF16)], inputs="v" * 11, cost=40_000_000_000)(
        low, base, factor, low_node, metric, coeffs, here_low, away_low, here_map, away_map, inner
    )
    far = lax.ppermute(surface, ("comp", "tile"), crossed(away))
    near = lax.ppermute(surface, ("comp", "tile"), crossed(here))
    own = lax.ppermute(surface, ("comp", "tile"), crossed(straight))
    (nxt,) = call(
        finish_kernel,
        [((1024, 512), F32)],
        [
            pltpu.VMEM((4, 1024, 128), F32), pltpu.VMEM((1024, 512), F32), pltpu.VMEM((256, 1024), BF16),
            pltpu.SemaphoreType.DMA((4,)),
        ],
        "v" * 12, "h",
    )(chunks, part, here_edge, away_edge, here_map, away_map, inner, weights, metric, coeffs, sea_mask, forcing)
    (new_forcing,) = call(
        remap_kernel, [(forcing.shape, F32)], [pltpu.VMEM((4 * slots, 128), F32)], "v" * 6,
    )(own, near, far, pick, total, remap_weights[0])
    return nxt.reshape(state.shape), new_forcing


def solution(mesh):
    placed = (
        P("comp", None, None, None, "tile"),
        P("comp", "tile"),
        P("comp", None, None),
        P("comp", None, None),
        P("comp", None),
        P("comp", "tile"),
        P("comp", None, "tile"),
        P("comp", None, None, "tile"),
        P("comp", "tile", None, None),
        P("comp", "tile"),
        P("comp", "tile"),
    )
    return jax.shard_map(
        shards,
        mesh=mesh,
        in_specs=placed,
        out_specs=(P("comp", None, None, None, "tile"), P("comp", None, None, "tile")),
        check_vma=False,
    )
```

```python
import functools

import jax
import jax.numpy as jnp
import numpy as np
from jax import lax
from jax.experimental import pallas as pl
from jax.experimental.pallas import tpu as pltpu
from jax.sharding import PartitionSpec as P

F32 = jnp.float32
BF16 = jnp.bfloat16
VMEM_LIMIT = 40 * 1024 * 1024


def dot(a, b):
    return jnp.dot(a, b, preferred_element_type=F32)


def iota(shape, dim):
    return lax.broadcasted_iota(jnp.int32, shape, dim)


def ends():
    here = jnp.where(lax.rem(lax.axis_index("tile"), 2) == 0, 12, 0)
    return here, 12 - here


def group_node(group, place):
    here, away = ends()
    side = jnp.where(group == 2, 4 * place + 3, 4 * place)
    return jnp.where(group == 0, here + place, jnp.where(group == 1, away + place, side))


def spread_matrix():
    col = iota((256, 256), 1)
    wanted = (col % 16) * 16 + group_node(col // 64, 3 - col // 16 % 4)
    return (iota((256, 256), 0) == wanted).astype(BF16)


def coupling_matrices(node_ref, level_ref):
    rows, cols = iota((16, 256), 0), iota((16, 256), 1)
    inner, outer = (cols % 16 == rows).astype(BF16), (cols // 16 == rows).astype(BF16)
    r, c = iota((256, 256), 0), iota((256, 256), 1)
    node = jnp.concatenate([dot(node_ref[0].astype(BF16), inner)] * 16, axis=0)
    node = jnp.where(r // 16 == c // 16, node, 0.0).astype(BF16)
    level = dot(level_ref[0].astype(BF16), outer)
    level = jnp.concatenate([jnp.broadcast_to(level[l : l + 1], (16, 256)) for l in range(16)], axis=0)
    level = jnp.where(r % 16 == c % 16, level, 0.0).astype(BF16)
    return node, level


def diagonal(metric, penalty):
    node = iota((16, metric.shape[1]), 0)
    i, j = node // 4, node % 4
    edges = ((i == 0) | (i == 3)).astype(F32) + ((j == 0) | (j == 3)).astype(F32)
    return 0.8 - 0.3 * metric - penalty * edges


def exchange_rate(coeffs_ref, mask):
    mask = mask.astype(F32)
    return coeffs_ref[:, 1:2] * mask + coeffs_ref[:, 2:3] * (1.0 - mask)


def levels_of(pattern):
    return jnp.concatenate([pattern] * 16, axis=0)


def halves(value):
    high = value.astype(BF16)
    return high, (value - high.astype(F32)).astype(BF16)


def low_select():
    row = iota((64, 64), 0)
    wanted = (row % 16 // 4) * 16 + group_node(row // 16, row % 4)
    return (iota((64, 64), 1) == wanted).astype(BF16)


def low_spread(first, second):
    col = iota((64, 64), 1)
    wanted = (col % 16 // 4) * 16 + group_node(jnp.where(col < 32, first, second), 3 - col % 4)
    return (iota((64, 64), 0) == wanted).astype(BF16)


def low_node_matrix(node):
    row, col = iota((64, 64), 0), iota((64, 64), 1)
    rows_of = (iota((64, 16), 0) % 16 == iota((64, 16), 1)).astype(BF16)
    cols_of = (iota((16, 64), 1) % 16 == iota((16, 64), 0)).astype(BF16)
    parts = [dot(dot(rows_of, part).astype(BF16), cols_of) for part in halves(node)]
    high, low = [jnp.where(row // 16 == col // 16, part, 0.0).astype(BF16) for part in parts]
    return jnp.concatenate([high, high, low], axis=1)


def low_node_product(matrix, value):
    high, low = halves(value)
    return dot(matrix, jnp.concatenate([high, low, high], axis=0))


LANES = [slice(128 * c, 128 * (c + 1)) for c in range(4)]
SIDE_NODES = ((3, 7, 11, 15), (0, 4, 8, 12))


def whole_rows(ref, start, count):
    return jnp.concatenate([ref[c, start : start + count, :] for c in range(4)], axis=1)


def mix_to_lowest(level, ref):
    parts = []
    for v in range(4):
        total = level[0, 0, 0] * whole_rows(ref, 256 * v, 16)
        for m in range(1, 16):
            total = total + level[0, 0, m] * whole_rows(ref, 256 * v + 16 * m, 16)
        parts.append(total)
    return jnp.concatenate(parts, axis=0)


def pack_node(ref, v, c, node, scale):
    return (scale * ref[c, pl.ds(256 * v + node, 16, stride=16), :]).astype(BF16)


def pack_facing(ref, scale, here_ref, away_ref, start):
    for target, first in zip((here_ref, away_ref), ends()):
        for v in range(4):
            for place in range(4):
                at = start + 64 * v + 16 * place
                for c in range(4):
                    target[at : at + 16, LANES[c]] = pack_node(ref, v, c, first + place, scale)


def pack_sides(ref, scale, edges):
    for side in range(2):
        for v in range(4):
            for place in range(4):
                at = 64 * v + 16 * place
                for c in range(4):
                    lanes = slice(512 * side + 128 * c, 512 * side + 128 * (c + 1))
                    edges[at : at + 16, lanes] = pack_node(ref, v, c, SIDE_NODES[side][place], scale)


def first_kernel(state_hbm, partner_hbm, coeffs_hbm, state_ref, here_ref, away_ref, inner_ref, partner_ref, coeffs_ref, sems):
    pairs = [(partner_hbm, partner_ref), (coeffs_hbm, coeffs_ref)]
    pairs += [(state_hbm.at[:, LANES[c]], state_ref.at[c]) for c in range(4)]
    copies = [pltpu.make_async_copy(source, target, sems.at[i]) for i, (source, target) in enumerate(pairs)]
    for copy in copies:
        copy.start()
    copies[0].wait()
    for step in range(4):
        columns = partner_ref[0:1, 512 + 256 * step : 768 + 256 * step] - 1024
        hit = iota((1024, 256), 0) == columns
        inner_ref[:, 256 * step : 256 * (step + 1)] = jnp.where(hit, 1.0, 0.0).astype(BF16)
    for copy in copies[1:]:
        copy.wait()
    pack_facing(state_ref, coeffs_ref[0, 0], here_ref, away_ref, 0)


def local_kernel(
    state_ref, inner_ref, metric_ref, node_ref, level_ref, coeffs_ref, mask_ref, forcing_ref, order_ref,
    part_ref, here_ref, away_ref, here_low_ref, away_low_ref,
    weights_ref, low_ref, base_ref, factor_ref, low_node_ref,
    level_smem, edges, sem,
):
    scalars = pltpu.make_async_copy(level_ref, level_smem, sem)
    scalars.start()
    select_low, spread_inner = low_select(), low_spread(2, 3)
    weights_ref[:, 512:768] = spread_matrix()
    penalty = coeffs_ref[:, 0:1]
    metric = metric_ref[...]
    node, level = coupling_matrices(node_ref, level_ref)
    weights_ref[:, 0:256] = node
    weights_ref[:, 256:512] = level
    low_node = low_node_matrix(node_ref[0])
    low_node_ref[...] = low_node
    factor = diagonal(metric, penalty)
    pack_sides(state_ref, penalty, edges)
    lowest = jnp.concatenate([whole_rows(state_ref, 256 * v, 16) for v in range(4)], axis=0)
    high, low = [dot(select_low, part).astype(BF16) for part in halves(penalty * lowest)]
    here_low_ref[0:16, :] = high[0:16]
    here_low_ref[16:32, :] = low[0:16]
    away_low_ref[0:16, :] = high[16:32]
    away_low_ref[16:32, :] = low[16:32]
    edges[256:272, 0:512] = high[32:48]
    edges[256:272, 512:1024] = high[48:64]
    edges[272:288, 0:512] = low[32:48]
    edges[272:288, 512:1024] = low[48:64]
    moved = dot(edges[...], inner_ref[...]).astype(BF16)
    rate = exchange_rate(coeffs_ref, mask_ref[0])
    rates = jnp.concatenate([rate] * 4, axis=0)
    forced = rates * jnp.concatenate([forcing_ref[0, v] for v in range(4)], axis=0)
    factor_low = factor - rate
    factor_ref[...] = factor_low
    scalars.wait()
    mixed = mix_to_lowest(level_smem, state_ref)
    near = moved[256:288]
    p_low = jnp.concatenate([factor_low] * 4, axis=0) * lowest + forced + mixed
    p_low = p_low + low_node_product(low_node, lowest * metric)
    p_low = p_low + dot(spread_inner, jnp.concatenate([near[:, 0:512], near[:, 512:1024]], axis=0))
    low_ref[...] = p_low
    high, low = [dot(select_low[0:32], part).astype(BF16) for part in halves(penalty * (p_low + mixed))]
    here_low_ref[32:48, :] = high[0:16]
    here_low_ref[48:64, :] = low[0:16]
    away_low_ref[32:48, :] = high[16:32]
    away_low_ref[48:64, :] = low[16:32]
    factors = levels_of(factor)
    for v in range(4):
        u = whole_rows(state_ref, 256 * v, 256)
        operand = [(u * metric).astype(BF16), u.astype(BF16)]
        operand += [moved[64 * v : 64 * (v + 1), 512 * side : 512 * (side + 1)] for side in range(2)]
        p = dot(jnp.concatenate([weights_ref[:, 0:512], weights_ref[:, 640:768]], axis=1), jnp.concatenate(operand, axis=0))
        p = jnp.concatenate([p_low[16 * v : 16 * (v + 1)], (factors * u + p)[16:256]], axis=0)
        for c in range(4):
            part_ref[c, 256 * v : 256 * (v + 1), :] = p[:, LANES[c]]
    pack_facing(part_ref, penalty, here_ref, away_ref, 0)
    mixed = mix_to_lowest(level_smem, part_ref)
    node_at = iota((64, 1), 0) % 16
    facing = jnp.where((node_at // 4 == 0) | (node_at // 4 == 3), penalty * penalty, 0.0)
    base_ref[...] = mixed + forced + facing * lowest


def lowest_kernel(
    low_ref, base_ref, factor_ref, low_node_ref, metric_ref, coeffs_ref, here_ref, away_ref, here_map, away_map, inner_ref,
    order_ref, surface_ref,
):
    penalty = coeffs_ref[:, 0:1]
    here = dot(here_ref[...], here_map[...]).astype(BF16)
    away = dot(away_ref[...], away_map[...]).astype(BF16)
    outer, inner, select = low_spread(0, 1), low_spread(2, 3), low_select()
    u1 = low_ref[...] + dot(outer, jnp.concatenate([here[0:32], away[0:32]], axis=0))
    high, low = [dot(select[32:64], part).astype(BF16) for part in halves(penalty * u1)]
    sides = [jnp.concatenate([high[at : at + 16], low[at : at + 16]], axis=0) for at in (0, 16)]
    near = dot(jnp.concatenate(sides, axis=1), inner_ref[...]).astype(BF16)
    x = base_ref[...] + jnp.concatenate([factor_ref[...]] * 4, axis=0) * u1
    x = x + low_node_product(low_node_ref[...], u1 * metric_ref[...])
    x = x + dot(outer, jnp.concatenate([here[32:64], away[32:64]], axis=0))
    x = x + dot(inner, jnp.concatenate([near[:, 0:512], near[:, 512:1024]], axis=0))
    x = x.astype(BF16)
    for v in range(4):
        for q in range(4):
            surface_ref[64 * v + 16 * q : 64 * v + 16 * (q + 1), :] = x[16 * v : 16 * (v + 1), 128 * q : 128 * (q + 1)]


def tables_kernel(
    partner_ref, rows_ref, cols_ref, here_map, away_map, pick_ref, sum_ref,
):
    last = ends()[0] == 12
    before, after = partner_ref[0:1, 0:512], partner_ref[0:1, 1536:2048] - 2560
    here_map[...] = jnp.where(iota((512, 512), 0) == jnp.where(last, after, before), 1.0, 0.0).astype(BF16)
    away_map[...] = jnp.where(iota((512, 512), 0) == jnp.where(last, before, after), 1.0, 0.0).astype(BF16)
    odd = lax.rem(lax.axis_index("tile"), 2)
    slots = rows_ref.shape[1]
    wide = 4 * slots
    repeat = (iota((slots, wide), 1) // 4 == iota((slots, wide), 0)).astype(BF16)
    widen = lambda ref: dot(jnp.broadcast_to(ref[0:1, :].astype(BF16), (16, slots)), repeat)[0:1].astype(jnp.int32)
    rows, cols = widen(rows_ref), widen(cols_ref)
    tile, block = cols // 64, cols % 64
    tile = jnp.where(odd == 1, 2 - tile, tile)
    var = iota((1, wide), 1) % 4
    wanted = tile * 256 + var * 64 + (block % 4) * 16 + block // 4
    pick_ref[...] = jnp.transpose((iota((768, wide), 0) == wanted).astype(F32)).astype(BF16)
    wanted = jnp.where(rows == 64, -1, var * 64 + (rows % 4) * 16 + rows // 4)
    sum_ref[...] = (iota((256, wide), 0) == wanted).astype(BF16)


def finish_kernel(
    state_ref, part_ref, here_first, away_first, here_ref, away_ref, here_map, away_map, inner_ref, weights_ref,
    metric_ref, coeffs_ref, mask_ref, forcing_ref,
    next_hbm, middle_ref, next_ref, edges, sems,
):
    penalty = coeffs_ref[:, 0:1]
    metric = metric_ref[...]
    here = dot(jnp.concatenate([here_first[...], here_ref[...]], axis=0), here_map[...]).astype(BF16)
    away = dot(jnp.concatenate([away_first[...], away_ref[...]], axis=0), away_map[...]).astype(BF16)
    for v in range(4):
        rows = slice(64 * v, 64 * (v + 1))
        halo = dot(weights_ref[:, 512:640], jnp.concatenate([here[rows], away[rows]], axis=0))
        for c in range(4):
            middle_ref[c, 256 * v : 256 * (v + 1), :] = part_ref[c, 256 * v : 256 * (v + 1), :] + halo[:, LANES[c]]
    pack_sides(middle_ref, penalty, edges)
    moved = dot(edges[...], inner_ref[...]).astype(BF16)
    factors = levels_of(diagonal(metric, penalty))
    node = iota((256, 1), 0) % 16
    facing = jnp.where((node // 4 == 0) | (node // 4 == 3), penalty * penalty, 0.0)
    rate = exchange_rate(coeffs_ref, mask_ref[0])
    copies = []
    for v in range(4):
        u1 = whole_rows(middle_ref, 256 * v, 256)
        rows = slice(64 * v, 64 * (v + 1))
        far = slice(256 + 64 * v, 256 + 64 * (v + 1))
        operand = [(u1 * metric).astype(BF16), u1.astype(BF16), here[far], away[far]]
        operand += [moved[rows, 512 * side : 512 * (side + 1)] for side in range(2)]
        x = factors * u1 + facing * whole_rows(state_ref, 256 * v, 256)
        x = x + dot(weights_ref[...], jnp.concatenate(operand, axis=0))
        added = rate * (forcing_ref[0, v] - u1[0:16])
        next_ref[256 * v : 256 * (v + 1), :] = jnp.concatenate([x[0:16] + added, x[16:256]], axis=0)
        rows = pl.ds(256 * v, 256)
        copies.append(pltpu.make_async_copy(next_ref.at[rows], next_hbm.at[rows], sems.at[v]))
        copies[-1].start()
    for copy in copies:
        copy.wait()


def remap_kernel(own_ref, near_ref, far_ref, pick_ref, sum_ref, blocks_ref, out_ref, products):
    picked = dot(pick_ref[:, 0:256], far_ref[...])
    picked = picked + dot(pick_ref[:, 256:512], own_ref[...])
    picked = picked + dot(pick_ref[:, 512:768], near_ref[...])
    slots = blocks_ref.shape[0]
    for quad in range(slots // 4):
        part = picked[16 * quad : 16 * (quad + 1)]
        upper = iota((16, 1), 0) % 8 < 4
        left = jnp.concatenate([jnp.where(upper, part, 0.0), jnp.where(upper, 0.0, part)], axis=1).astype(BF16)
        right = [jnp.concatenate([blocks_ref[4 * quad + 2 * h], blocks_ref[4 * quad + 2 * h + 1]], axis=1) for h in range(2)]
        both = lax.dot_general(
            left, jnp.concatenate(right, axis=0), (((1,), (1,)), ((), ())), preferred_element_type=F32
        )
        products[16 * quad : 16 * quad + 8, :] = both[0:8, 0:128]
        products[16 * quad + 8 : 16 * (quad + 1), :] = both[8:16, 128:256]
    value = products[...]
    high = value.astype(BF16)
    low = (value - high.astype(F32)).astype(BF16)
    total = dot(sum_ref[...], high) + dot(sum_ref[...], low)
    for v in range(4):
        for q in range(4):
            out_ref[0, v, :, 128 * q : 128 * (q + 1)] = total[64 * v + 16 * q : 64 * v + 16 * (q + 1)]


def call(kernel, outs, scratch=(), inputs="", results="", aliases={}, cost=0):
    spaces = {"v": pltpu.VMEM, "s": pltpu.SMEM, "h": pltpu.HBM, "a": pl.ANY}
    place = lambda kind: pl.BlockSpec(memory_space=spaces[kind])
    results = results or "v" * len(outs)
    return pl.pallas_call(
        kernel,
        out_shape=[jax.ShapeDtypeStruct(shape, kind) for shape, kind in outs],
        in_specs=[place(kind) for kind in inputs],
        out_specs=[place(kind) for kind in results],
        input_output_aliases=aliases,
        scratch_shapes=list(scratch),
        cost_estimate=pl.CostEstimate(flops=cost, bytes_accessed=0, transcendentals=0) if cost else None,
        compiler_params=pltpu.CompilerParams(vmem_limit_bytes=VMEM_LIMIT),
    )


def shards(
    state, metric, element_coupling, level_coupling, coeffs, edge_partner, sea_mask, forcing,
    remap_weights, remap_rows, remap_cols,
):
    tiles = lax.axis_size("tile")
    here = [(t, t ^ 1) for t in range(tiles)]
    away = [(t, (t + 1) % tiles if t % 2 else (t - 1) % tiles) for t in range(tiles)]
    crossed = lambda pairs: [(c * tiles + a, (1 - c) * tiles + b) for c in range(2) for a, b in pairs]
    straight = [(t, t) for t in range(tiles)]
    flat = state.reshape(1024, 512)
    hbm = lambda *values: [pltpu.with_memory_space_constraint(value, pltpu.HBM) for value in values]
    chunks, here_first, away_first, inner = call(
        first_kernel,
        [((4, 1024, 128), F32), ((256, 512), BF16), ((256, 512), BF16), ((1024, 1024), BF16)],
        [pltpu.VMEM(edge_partner.shape, jnp.int32), pltpu.SMEM(coeffs.shape, F32), pltpu.SemaphoreType.DMA((6,))],
        "hhh",
    )(*hbm(flat, edge_partner, coeffs))
    away_first = lax.ppermute(away_first, "tile", away)
    here_first = lax.ppermute(here_first, "tile", here)
    inputs = (metric, element_coupling, level_coupling, coeffs, sea_mask, forcing)
    (part, here_edge, away_edge, here_low, away_low, weights, low, base, factor, low_node) = call(
        local_kernel,
        [
            ((4, 1024, 128), F32), ((256, 512), BF16), ((256, 512), BF16), ((64, 512), BF16),
            ((64, 512), BF16), ((256, 768), BF16),
            ((64, 512), F32), ((64, 512), F32), ((16, 512), F32), ((64, 192), BF16),
        ],
        [pltpu.SMEM((1, 16, 16), F32), pltpu.VMEM((288, 1024), BF16), pltpu.SemaphoreType.DMA],
        "v" * 8 + "a",
    )(chunks, inner, *inputs, here_first)
    away_low = lax.ppermute(away_low, "tile", away)
    here_low = lax.ppermute(here_low, "tile", here)
    slots = remap_rows.shape[1]
    here_map, away_map, pick, total = call(
        tables_kernel,
        [
            ((512, 512), BF16), ((512, 512), BF16), ((4 * slots, 768), BF16), ((256, 4 * slots), BF16),
        ],
        inputs="vvv", results="vvvv", cost=4_000_000_000,
    )(edge_partner, remap_rows, remap_cols)
    away_edge = lax.ppermute(away_edge, "tile", away)
    here_edge = lax.ppermute(here_edge, "tile", here)
    (surface,) = call(lowest_kernel, [((256, 128), BF16)], inputs="v" * 11 + "a", cost=40_000_000_000)(
        low, base, factor, low_node, metric, coeffs, here_low, away_low, here_map, away_map, inner, here_edge
    )
    far = lax.ppermute(surface, ("comp", "tile"), crossed(away))
    near = lax.ppermute(surface, ("comp", "tile"), crossed(here))
    own = lax.ppermute(surface, ("comp", "tile"), crossed(straight))
    (nxt,) = call(
        finish_kernel,
        [((1024, 512), F32)],
        [
            pltpu.VMEM((4, 1024, 128), F32), pltpu.VMEM((1024, 512), F32), pltpu.VMEM((256, 1024), BF16),
            pltpu.SemaphoreType.DMA((4,)),
        ],
        "v" * 14, "h",
    )(chunks, part, here_first, away_first, here_edge, away_edge, here_map, away_map, inner, weights, metric, coeffs, sea_mask, forcing)
    (new_forcing,) = call(
        remap_kernel, [(forcing.shape, F32)], [pltpu.VMEM((4 * slots, 128), F32)], "v" * 6,
    )(own, near, far, pick, total, remap_weights[0])
    return nxt.reshape(state.shape), new_forcing


def solution(mesh):
    placed = (
        P("comp", None, None, None, "tile"),
        P("comp", "tile"),
        P("comp", None, None),
        P("comp", None, None),
        P("comp", None),
        P("comp", "tile"),
        P("comp", None, "tile"),
        P("comp", None, None, "tile"),
        P("comp", "tile", None, None),
        P("comp", "tile"),
        P("comp", "tile"),
    )
    return jax.shard_map(
        shards,
        mesh=mesh,
        in_specs=placed,
        out_specs=(P("comp", None, None, None, "tile"), P("comp", None, None, "tile")),
        check_vma=False,
    )
```

```python
import functools

import jax
import jax.numpy as jnp
import numpy as np
from jax import lax
from jax.experimental import pallas as pl
from jax.experimental.pallas import tpu as pltpu
from jax.sharding import PartitionSpec as P

F32 = jnp.float32
BF16 = jnp.bfloat16
VMEM_LIMIT = 40 * 1024 * 1024


def dot(a, b):
    return jnp.dot(a, b, preferred_element_type=F32)


def iota(shape, dim):
    return lax.broadcasted_iota(jnp.int32, shape, dim)


def ends():
    here = jnp.where(lax.rem(lax.axis_index("tile"), 2) == 0, 12, 0)
    return here, 12 - here


def group_node(group, place):
    here, away = ends()
    side = jnp.where(group == 2, 4 * place + 3, 4 * place)
    return jnp.where(group == 0, here + place, jnp.where(group == 1, away + place, side))


def spread_matrix():
    col = iota((256, 256), 1)
    wanted = (col % 16) * 16 + group_node(col // 64, 3 - col // 16 % 4)
    return (iota((256, 256), 0) == wanted).astype(BF16)


def coupling_matrices(node_ref, level_ref):
    rows, cols = iota((16, 256), 0), iota((16, 256), 1)
    inner, outer = (cols % 16 == rows).astype(BF16), (cols // 16 == rows).astype(BF16)
    r, c = iota((256, 256), 0), iota((256, 256), 1)
    both = []
    for part in halves(node_ref[0]):
        node = jnp.concatenate([dot(part, inner)] * 16, axis=0)
        both.append(jnp.where(r // 16 == c // 16, node, 0.0).astype(BF16))
    for part in halves(level_ref[0]):
        level = dot(part, outer)
        level = jnp.concatenate([jnp.broadcast_to(level[l : l + 1], (16, 256)) for l in range(16)], axis=0)
        both.append(jnp.where(r % 16 == c % 16, level, 0.0).astype(BF16))
    return both[0], both[2], both[1], both[3]


def diagonal(metric, penalty):
    node = iota((16, metric.shape[1]), 0)
    i, j = node // 4, node % 4
    edges = ((i == 0) | (i == 3)).astype(F32) + ((j == 0) | (j == 3)).astype(F32)
    return 0.8 - 0.3 * metric - penalty * edges


def exchange_rate(coeffs_ref, mask):
    mask = mask.astype(F32)
    return coeffs_ref[:, 1:2] * mask + coeffs_ref[:, 2:3] * (1.0 - mask)


def levels_of(pattern):
    return jnp.concatenate([pattern] * 16, axis=0)


def halves(value):
    high = value.astype(BF16)
    return high, (value - high.astype(F32)).astype(BF16)


def low_select():
    row = iota((64, 64), 0)
    wanted = (row % 16 // 4) * 16 + group_node(row // 16, row % 4)
    return (iota((64, 64), 1) == wanted).astype(BF16)


def low_spread(first, second):
    col = iota((64, 64), 1)
    wanted = (col % 16 // 4) * 16 + group_node(jnp.where(col < 32, first, second), 3 - col % 4)
    return (iota((64, 64), 0) == wanted).astype(BF16)


def low_node_matrix(node):
    row, col = iota((64, 64), 0), iota((64, 64), 1)
    rows_of = (iota((64, 16), 0) % 16 == iota((64, 16), 1)).astype(BF16)
    cols_of = (iota((16, 64), 1) % 16 == iota((16, 64), 0)).astype(BF16)
    parts = [dot(dot(rows_of, part).astype(BF16), cols_of) for part in halves(node)]
    high, low = [jnp.where(row // 16 == col // 16, part, 0.0).astype(BF16) for part in parts]
    return jnp.concatenate([high, high, low], axis=1)


def low_node_product(matrix, value):
    high, low = halves(value)
    return dot(matrix, jnp.concatenate([high, low, high], axis=0))


LANES = [slice(128 * c, 128 * (c + 1)) for c in range(4)]
SIDE_NODES = ((3, 7, 11, 15), (0, 4, 8, 12))


def whole_rows(ref, start, count):
    return jnp.concatenate([ref[c, start : start + count, :] for c in range(4)], axis=1)


def mix_to_lowest(level, ref):
    parts = []
    for v in range(4):
        total = level[0, 0, 0] * whole_rows(ref, 256 * v, 16)
        for m in range(1, 16):
            total = total + level[0, 0, m] * whole_rows(ref, 256 * v + 16 * m, 16)
        parts.append(total)
    return jnp.concatenate(parts, axis=0)


def pack_node(ref, v, c, node, scale):
    return (scale * ref[c, pl.ds(256 * v + node, 16, stride=16), :]).astype(BF16)


def pack_facing(ref, scale, here_ref, away_ref, start):
    for target, first in zip((here_ref, away_ref), ends()):
        for v in range(4):
            for place in range(4):
                at = start + 64 * v + 16 * place
                for c in range(4):
                    target[at : at + 16, LANES[c]] = pack_node(ref, v, c, first + place, scale)


def pack_sides(ref, scale, edges):
    for side in range(2):
        for v in range(4):
            for place in range(4):
                at = 64 * v + 16 * place
                for c in range(4):
                    lanes = slice(512 * side + 128 * c, 512 * side + 128 * (c + 1))
                    edges[at : at + 16, lanes] = pack_node(ref, v, c, SIDE_NODES[side][place], scale)


def first_kernel(state_hbm, partner_hbm, coeffs_hbm, state_ref, here_ref, away_ref, inner_ref, partner_ref, coeffs_ref, sems):
    pairs = [(partner_hbm, partner_ref), (coeffs_hbm, coeffs_ref)]
    pairs += [(state_hbm.at[:, LANES[c]], state_ref.at[c]) for c in range(4)]
    copies = [pltpu.make_async_copy(source, target, sems.at[i]) for i, (source, target) in enumerate(pairs)]
    for copy in copies:
        copy.start()
    copies[0].wait()
    for step in range(4):
        columns = partner_ref[0:1, 512 + 256 * step : 768 + 256 * step] - 1024
        hit = iota((1024, 256), 0) == columns
        inner_ref[:, 256 * step : 256 * (step + 1)] = jnp.where(hit, 1.0, 0.0).astype(BF16)
    for copy in copies[1:]:
        copy.wait()
    pack_facing(state_ref, coeffs_ref[0, 0], here_ref, away_ref, 0)


def local_kernel(
    state_ref, inner_ref, metric_ref, node_ref, level_ref, coeffs_ref, mask_ref, forcing_ref, order_ref,
    part_ref, here_ref, away_ref, here_low_ref, away_low_ref,
    weights_ref, low_ref, base_ref, factor_ref, low_node_ref,
    level_smem, edges, sem,
):
    scalars = pltpu.make_async_copy(level_ref, level_smem, sem)
    scalars.start()
    select_low, spread_inner = low_select(), low_spread(2, 3)
    weights_ref[:, 512:768] = spread_matrix()
    penalty = coeffs_ref[:, 0:1]
    metric = metric_ref[...]
    for part, start in zip(coupling_matrices(node_ref, level_ref), (0, 256, 768, 1024)):
        weights_ref[:, start : start + 256] = part
    low_node = low_node_matrix(node_ref[0])
    low_node_ref[...] = low_node
    factor = diagonal(metric, penalty)
    pack_sides(state_ref, penalty, edges)
    lowest = jnp.concatenate([whole_rows(state_ref, 256 * v, 16) for v in range(4)], axis=0)
    high, low = [dot(select_low, part).astype(BF16) for part in halves(penalty * lowest)]
    here_low_ref[0:16, :] = high[0:16]
    here_low_ref[16:32, :] = low[0:16]
    away_low_ref[0:16, :] = high[16:32]
    away_low_ref[16:32, :] = low[16:32]
    edges[256:272, 0:512] = high[32:48]
    edges[256:272, 512:1024] = high[48:64]
    edges[272:288, 0:512] = low[32:48]
    edges[272:288, 512:1024] = low[48:64]
    moved = dot(edges[...], inner_ref[...]).astype(BF16)
    rate = exchange_rate(coeffs_ref, mask_ref[0])
    rates = jnp.concatenate([rate] * 4, axis=0)
    forced = rates * jnp.concatenate([forcing_ref[0, v] for v in range(4)], axis=0)
    factor_low = factor - rate
    factor_ref[...] = factor_low
    scalars.wait()
    mixed = mix_to_lowest(level_smem, state_ref)
    near = moved[256:288]
    p_low = jnp.concatenate([factor_low] * 4, axis=0) * lowest + forced + mixed
    p_low = p_low + low_node_product(low_node, lowest * metric)
    p_low = p_low + dot(spread_inner, jnp.concatenate([near[:, 0:512], near[:, 512:1024]], axis=0))
    low_ref[...] = p_low
    high, low = [dot(select_low[0:32], part).astype(BF16) for part in halves(penalty * (p_low + mixed))]
    here_low_ref[32:48, :] = high[0:16]
    here_low_ref[48:64, :] = low[0:16]
    away_low_ref[32:48, :] = high[16:32]
    away_low_ref[48:64, :] = low[16:32]
    factors = levels_of(factor)
    for v in range(4):
        u = whole_rows(state_ref, 256 * v, 256)
        operand = [(u * metric).astype(BF16), u.astype(BF16)]
        operand += [moved[64 * v : 64 * (v + 1), 512 * side : 512 * (side + 1)] for side in range(2)]
        operand += operand[0:2]
        p = dot(jnp.concatenate([weights_ref[:, 0:512], weights_ref[:, 640:1280]], axis=1), jnp.concatenate(operand, axis=0))
        p = jnp.concatenate([p_low[16 * v : 16 * (v + 1)], (factors * u + p)[16:256]], axis=0)
        for c in range(4):
            part_ref[c, 256 * v : 256 * (v + 1), :] = p[:, LANES[c]]
    pack_facing(part_ref, penalty, here_ref, away_ref, 0)
    mixed = mix_to_lowest(level_smem, part_ref)
    node_at = iota((64, 1), 0) % 16
    facing = jnp.where((node_at // 4 == 0) | (node_at // 4 == 3), penalty * penalty, 0.0)
    base_ref[...] = mixed + forced + facing * lowest


def lowest_kernel(
    low_ref, base_ref, factor_ref, low_node_ref, metric_ref, coeffs_ref, here_ref, away_ref, here_map, away_map, inner_ref,
    order_ref, surface_ref,
):
    penalty = coeffs_ref[:, 0:1]
    here = dot(here_ref[...], here_map[...]).astype(BF16)
    away = dot(away_ref[...], away_map[...]).astype(BF16)
    outer, inner, select = low_spread(0, 1), low_spread(2, 3), low_select()
    u1 = low_ref[...] + dot(outer, jnp.concatenate([here[0:32], away[0:32]], axis=0))
    high, low = [dot(select[32:64], part).astype(BF16) for part in halves(penalty * u1)]
    sides = [jnp.concatenate([high[at : at + 16], low[at : at + 16]], axis=0) for at in (0, 16)]
    near = dot(jnp.concatenate(sides, axis=1), inner_ref[...]).astype(BF16)
    x = base_ref[...] + jnp.concatenate([factor_ref[...]] * 4, axis=0) * u1
    x = x + low_node_product(low_node_ref[...], u1 * metric_ref[...])
    x = x + dot(outer, jnp.concatenate([here[32:64], away[32:64]], axis=0))
    x = x + dot(inner, jnp.concatenate([near[:, 0:512], near[:, 512:1024]], axis=0))
    x = x.astype(BF16)
    for v in range(4):
        for q in range(4):
            surface_ref[64 * v + 16 * q : 64 * v + 16 * (q + 1), :] = x[16 * v : 16 * (v + 1), 128 * q : 128 * (q + 1)]


def tables_kernel(
    partner_ref, rows_ref, cols_ref, here_map, away_map, pick_ref, sum_ref,
):
    last = ends()[0] == 12
    before, after = partner_ref[0:1, 0:512], partner_ref[0:1, 1536:2048] - 2560
    here_map[...] = jnp.where(iota((512, 512), 0) == jnp.where(last, after, before), 1.0, 0.0).astype(BF16)
    away_map[...] = jnp.where(iota((512, 512), 0) == jnp.where(last, before, after), 1.0, 0.0).astype(BF16)
    odd = lax.rem(lax.axis_index("tile"), 2)
    slots = rows_ref.shape[1]
    wide = 4 * slots
    repeat = (iota((slots, wide), 1) // 4 == iota((slots, wide), 0)).astype(BF16)
    widen = lambda ref: dot(jnp.broadcast_to(ref[0:1, :].astype(BF16), (16, slots)), repeat)[0:1].astype(jnp.int32)
    rows, cols = widen(rows_ref), widen(cols_ref)
    tile, block = cols // 64, cols % 64
    tile = jnp.where(odd == 1, 2 - tile, tile)
    var = iota((1, wide), 1) % 4
    wanted = tile * 256 + var * 64 + (block % 4) * 16 + block // 4
    pick_ref[...] = jnp.transpose((iota((768, wide), 0) == wanted).astype(F32)).astype(BF16)
    wanted = jnp.where(rows == 64, -1, var * 64 + (rows % 4) * 16 + rows // 4)
    sum_ref[...] = (iota((256, wide), 0) == wanted).astype(BF16)


def finish_kernel(
    state_ref, part_ref, here_first, away_first, here_ref, away_ref, here_map, away_map, inner_ref, weights_ref,
    metric_ref, coeffs_ref, mask_ref, forcing_ref,
    next_hbm, middle_ref, next_ref, edges, sems,
):
    penalty = coeffs_ref[:, 0:1]
    metric = metric_ref[...]
    here = dot(jnp.concatenate([here_first[...], here_ref[...]], axis=0), here_map[...]).astype(BF16)
    away = dot(jnp.concatenate([away_first[...], away_ref[...]], axis=0), away_map[...]).astype(BF16)
    for v in range(4):
        rows = slice(64 * v, 64 * (v + 1))
        halo = dot(weights_ref[:, 512:640], jnp.concatenate([here[rows], away[rows]], axis=0))
        for c in range(4):
            middle_ref[c, 256 * v : 256 * (v + 1), :] = part_ref[c, 256 * v : 256 * (v + 1), :] + halo[:, LANES[c]]
    pack_sides(middle_ref, penalty, edges)
    moved = dot(edges[...], inner_ref[...]).astype(BF16)
    factors = levels_of(diagonal(metric, penalty))
    node = iota((256, 1), 0) % 16
    facing = jnp.where((node // 4 == 0) | (node // 4 == 3), penalty * penalty, 0.0)
    rate = exchange_rate(coeffs_ref, mask_ref[0])
    copies = []
    for v in range(4):
        u1 = whole_rows(middle_ref, 256 * v, 256)
        rows = slice(64 * v, 64 * (v + 1))
        far = slice(256 + 64 * v, 256 + 64 * (v + 1))
        operand = [(u1 * metric).astype(BF16), u1.astype(BF16), here[far], away[far]]
        operand += [moved[rows, 512 * side : 512 * (side + 1)] for side in range(2)]
        operand += operand[0:2]
        x = factors * u1 + facing * whole_rows(state_ref, 256 * v, 256)
        x = x + dot(weights_ref[...], jnp.concatenate(operand, axis=0))
        added = rate * (forcing_ref[0, v] - u1[0:16])
        next_ref[256 * v : 256 * (v + 1), :] = jnp.concatenate([x[0:16] + added, x[16:256]], axis=0)
        rows = pl.ds(256 * v, 256)
        copies.append(pltpu.make_async_copy(next_ref.at[rows], next_hbm.at[rows], sems.at[v]))
        copies[-1].start()
    for copy in copies:
        copy.wait()


def remap_kernel(own_ref, near_ref, far_ref, pick_ref, sum_ref, blocks_ref, out_ref, products):
    picked = dot(pick_ref[:, 0:256], far_ref[...])
    picked = picked + dot(pick_ref[:, 256:512], own_ref[...])
    picked = picked + dot(pick_ref[:, 512:768], near_ref[...])
    slots = blocks_ref.shape[0]
    for quad in range(slots // 4):
        part = picked[16 * quad : 16 * (quad + 1)]
        upper = iota((16, 1), 0) % 8 < 4
        left = jnp.concatenate([jnp.where(upper, part, 0.0), jnp.where(upper, 0.0, part)], axis=1).astype(BF16)
        right = [jnp.concatenate([blocks_ref[4 * quad + 2 * h], blocks_ref[4 * quad + 2 * h + 1]], axis=1) for h in range(2)]
        both = lax.dot_general(
            left, jnp.concatenate(right, axis=0), (((1,), (1,)), ((), ())), preferred_element_type=F32
        )
        products[16 * quad : 16 * quad + 8, :] = both[0:8, 0:128]
        products[16 * quad + 8 : 16 * (quad + 1), :] = both[8:16, 128:256]
    value = products[...]
    high = value.astype(BF16)
    low = (value - high.astype(F32)).astype(BF16)
    total = dot(sum_ref[...], high) + dot(sum_ref[...], low)
    for v in range(4):
        for q in range(4):
            out_ref[0, v, :, 128 * q : 128 * (q + 1)] = total[64 * v + 16 * q : 64 * v + 16 * (q + 1)]


def call(kernel, outs, scratch=(), inputs="", results="", aliases={}, cost=0):
    spaces = {"v": pltpu.VMEM, "s": pltpu.SMEM, "h": pltpu.HBM, "a": pl.ANY}
    place = lambda kind: pl.BlockSpec(memory_space=spaces[kind])
    results = results or "v" * len(outs)
    return pl.pallas_call(
        kernel,
        out_shape=[jax.ShapeDtypeStruct(shape, kind) for shape, kind in outs],
        in_specs=[place(kind) for kind in inputs],
        out_specs=[place(kind) for kind in results],
        input_output_aliases=aliases,
        scratch_shapes=list(scratch),
        cost_estimate=pl.CostEstimate(flops=cost, bytes_accessed=0, transcendentals=0) if cost else None,
        compiler_params=pltpu.CompilerParams(vmem_limit_bytes=VMEM_LIMIT),
    )


def shards(
    state, metric, element_coupling, level_coupling, coeffs, edge_partner, sea_mask, forcing,
    remap_weights, remap_rows, remap_cols,
):
    tiles = lax.axis_size("tile")
    here = [(t, t ^ 1) for t in range(tiles)]
    away = [(t, (t + 1) % tiles if t % 2 else (t - 1) % tiles) for t in range(tiles)]
    crossed = lambda pairs: [(c * tiles + a, (1 - c) * tiles + b) for c in range(2) for a, b in pairs]
    straight = [(t, t) for t in range(tiles)]
    flat = state.reshape(1024, 512)
    hbm = lambda *values: [pltpu.with_memory_space_constraint(value, pltpu.HBM) for value in values]
    chunks, here_first, away_first, inner = call(
        first_kernel,
        [((4, 1024, 128), F32), ((256, 512), BF16), ((256, 512), BF16), ((1024, 1024), BF16)],
        [pltpu.VMEM(edge_partner.shape, jnp.int32), pltpu.SMEM(coeffs.shape, F32), pltpu.SemaphoreType.DMA((6,))],
        "hhh",
    )(*hbm(flat, edge_partner, coeffs))
    away_first = lax.ppermute(away_first, "tile", away)
    here_first = lax.ppermute(here_first, "tile", here)
    inputs = (metric, element_coupling, level_coupling, coeffs, sea_mask, forcing)
    (part, here_edge, away_edge, here_low, away_low, weights, low, base, factor, low_node) = call(
        local_kernel,
        [
            ((4, 1024, 128), F32), ((256, 512), BF16), ((256, 512), BF16), ((64, 512), BF16),
            ((64, 512), BF16), ((256, 1280), BF16),
            ((64, 512), F32), ((64, 512), F32), ((16, 512), F32), ((64, 192), BF16),
        ],
        [pltpu.SMEM((1, 16, 16), F32), pltpu.VMEM((288, 1024), BF16), pltpu.SemaphoreType.DMA],
        "v" * 8 + "a",
    )(chunks, inner, *inputs, here_first)
    away_low = lax.ppermute(away_low, "tile", away)
    here_low = lax.ppermute(here_low, "tile", here)
    slots = remap_rows.shape[1]
    here_map, away_map, pick, total = call(
        tables_kernel,
        [
            ((512, 512), BF16), ((512, 512), BF16), ((4 * slots, 768), BF16), ((256, 4 * slots), BF16),
        ],
        inputs="vvv", results="vvvv", cost=4_000_000_000,
    )(edge_partner, remap_rows, remap_cols)
    away_edge = lax.ppermute(away_edge, "tile", away)
    here_edge = lax.ppermute(here_edge, "tile", here)
    (surface,) = call(lowest_kernel, [((256, 128), BF16)], inputs="v" * 11 + "a", cost=40_000_000_000)(
        low, base, factor, low_node, metric, coeffs, here_low, away_low, here_map, away_map, inner, here_edge
    )
    far = lax.ppermute(surface, ("comp", "tile"), crossed(away))
    near = lax.ppermute(surface, ("comp", "tile"), crossed(here))
    own = lax.ppermute(surface, ("comp", "tile"), crossed(straight))
    (nxt,) = call(
        finish_kernel,
        [((1024, 512), F32)],
        [
            pltpu.VMEM((4, 1024, 128), F32), pltpu.VMEM((1024, 512), F32), pltpu.VMEM((256, 1024), BF16),
            pltpu.SemaphoreType.DMA((4,)),
        ],
        "v" * 14, "h",
    )(chunks, part, here_first, away_first, here_edge, away_edge, here_map, away_map, inner, weights, metric, coeffs, sea_mask, forcing)
    (new_forcing,) = call(
        remap_kernel, [(forcing.shape, F32)], [pltpu.VMEM((4 * slots, 128), F32)], "v" * 6,
    )(own, near, far, pick, total, remap_weights[0])
    return nxt.reshape(state.shape), new_forcing


def solution(mesh):
    placed = (
        P("comp", None, None, None, "tile"),
        P("comp", "tile"),
        P("comp", None, None),
        P("comp", None, None),
        P("comp", None),
        P("comp", "tile"),
        P("comp", None, "tile"),
        P("comp", None, None, "tile"),
        P("comp", "tile", None, None),
        P("comp", "tile"),
        P("comp", "tile"),
    )
    return jax.shard_map(
        shards,
        mesh=mesh,
        in_specs=placed,
        out_specs=(P("comp", None, None, None, "tile"), P("comp", None, None, "tile")),
        check_vma=False,
    )
```

```python
import functools

import jax
import jax.numpy as jnp
import numpy as np
from jax import lax
from jax.experimental import pallas as pl
from jax.experimental.pallas import tpu as pltpu
from jax.sharding import PartitionSpec as P

F32 = jnp.float32
BF16 = jnp.bfloat16
VMEM_LIMIT = 40 * 1024 * 1024


def dot(a, b):
    return jnp.dot(a, b, preferred_element_type=F32)


def iota(shape, dim):
    return lax.broadcasted_iota(jnp.int32, shape, dim)


def ends():
    here = jnp.where(lax.rem(lax.axis_index("tile"), 2) == 0, 12, 0)
    return here, 12 - here


def group_node(group, place):
    here, away = ends()
    side = jnp.where(group == 2, 4 * place + 3, 4 * place)
    return jnp.where(group == 0, here + place, jnp.where(group == 1, away + place, side))


def spread_matrix():
    col = iota((256, 256), 1)
    wanted = (col % 16) * 16 + group_node(col // 64, 3 - col // 16 % 4)
    return (iota((256, 256), 0) == wanted).astype(BF16)


def coupling_matrices(node_ref, level_ref):
    rows, cols = iota((16, 256), 0), iota((16, 256), 1)
    inner, outer = (cols % 16 == rows).astype(BF16), (cols // 16 == rows).astype(BF16)
    r, c = iota((256, 256), 0), iota((256, 256), 1)
    node = jnp.concatenate([dot(node_ref[0].astype(BF16), inner)] * 16, axis=0)
    node = jnp.where(r // 16 == c // 16, node, 0.0).astype(BF16)
    level = dot(level_ref[0].astype(BF16), outer)
    level = jnp.concatenate([jnp.broadcast_to(level[l : l + 1], (16, 256)) for l in range(16)], axis=0)
    level = jnp.where(r % 16 == c % 16, level, 0.0).astype(BF16)
    return node, level


def diagonal(metric, penalty):
    node = iota((16, metric.shape[1]), 0)
    i, j = node // 4, node % 4
    edges = ((i == 0) | (i == 3)).astype(F32) + ((j == 0) | (j == 3)).astype(F32)
    return 0.8 - 0.3 * metric - penalty * edges


def exchange_rate(coeffs_ref, mask):
    mask = mask.astype(F32)
    return coeffs_ref[:, 1:2] * mask + coeffs_ref[:, 2:3] * (1.0 - mask)


def levels_of(pattern):
    return jnp.concatenate([pattern] * 16, axis=0)


def halves(value):
    high = value.astype(BF16)
    return high, (value - high.astype(F32)).astype(BF16)


def low_select():
    row = iota((64, 64), 0)
    wanted = (row % 16 // 4) * 16 + group_node(row // 16, row % 4)
    return (iota((64, 64), 1) == wanted).astype(BF16)


def low_spread(first, second):
    col = iota((64, 64), 1)
    wanted = (col % 16 // 4) * 16 + group_node(jnp.where(col < 32, first, second), 3 - col % 4)
    return (iota((64, 64), 0) == wanted).astype(BF16)


def low_node_matrix(node):
    row, col = iota((64, 64), 0), iota((64, 64), 1)
    rows_of = (iota((64, 16), 0) % 16 == iota((64, 16), 1)).astype(BF16)
    cols_of = (iota((16, 64), 1) % 16 == iota((16, 64), 0)).astype(BF16)
    parts = [dot(dot(rows_of, part).astype(BF16), cols_of) for part in halves(node)]
    high, low = [jnp.where(row // 16 == col // 16, part, 0.0).astype(BF16) for part in parts]
    return jnp.concatenate([high, high, low], axis=1)


def low_node_product(matrix, value):
    high, low = halves(value)
    return dot(matrix, jnp.concatenate([high, low, high], axis=0))


LANES = [slice(128 * c, 128 * (c + 1)) for c in range(4)]
SIDE_NODES = ((3, 7, 11, 15), (0, 4, 8, 12))


def whole_rows(ref, start, count):
    return jnp.concatenate([ref[c, start : start + count, :] for c in range(4)], axis=1)


def mix_to_lowest(level, ref):
    parts = []
    for v in range(4):
        total = level[0, 0, 0] * whole_rows(ref, 256 * v, 16)
        for m in range(1, 16):
            total = total + level[0, 0, m] * whole_rows(ref, 256 * v + 16 * m, 16)
        parts.append(total)
    return jnp.concatenate(parts, axis=0)


def pack_node(ref, v, c, node, scale):
    return (scale * ref[c, pl.ds(256 * v + node, 16, stride=16), :]).astype(BF16)


def pack_facing(ref, scale, here_ref, away_ref, start):
    for target, first in zip((here_ref, away_ref), ends()):
        for v in range(4):
            for place in range(4):
                at = start + 64 * v + 16 * place
                for c in range(4):
                    target[at : at + 16, LANES[c]] = pack_node(ref, v, c, first + place, scale)


def pack_sides(ref, scale, edges):
    for side in range(2):
        for v in range(4):
            for place in range(4):
                at = 64 * v + 16 * place
                for c in range(4):
                    lanes = slice(512 * side + 128 * c, 512 * side + 128 * (c + 1))
                    edges[at : at + 16, lanes] = pack_node(ref, v, c, SIDE_NODES[side][place], scale)


def first_kernel(state_hbm, partner_hbm, coeffs_hbm, state_ref, here_ref, away_ref, inner_ref, spread_ref, partner_ref, coeffs_ref, sems):
    pairs = [(partner_hbm, partner_ref), (coeffs_hbm, coeffs_ref)]
    pairs += [(state_hbm.at[:, LANES[c]], state_ref.at[c]) for c in range(4)]
    copies = [pltpu.make_async_copy(source, target, sems.at[i]) for i, (source, target) in enumerate(pairs)]
    for copy in copies:
        copy.start()
    spread_ref[...] = spread_matrix()
    copies[0].wait()
    for step in range(4):
        columns = partner_ref[0:1, 512 + 256 * step : 768 + 256 * step] - 1024
        hit = iota((1024, 256), 0) == columns
        inner_ref[:, 256 * step : 256 * (step + 1)] = jnp.where(hit, 1.0, 0.0).astype(BF16)
    for copy in copies[1:]:
        copy.wait()
    pack_facing(state_ref, coeffs_ref[0, 0], here_ref, away_ref, 0)


def local_kernel(
    state_ref, inner_ref, spread_ref, metric_ref, node_ref, level_ref, coeffs_ref, mask_ref, forcing_ref, order_ref,
    part_ref, here_ref, away_ref, here_low_ref, away_low_ref,
    weights_ref, low_ref, base_ref, factor_ref, low_node_ref,
    level_smem, edges, sem,
):
    scalars = pltpu.make_async_copy(level_ref, level_smem, sem)
    scalars.start()
    select_low, spread_inner = low_select(), low_spread(2, 3)
    weights_ref[:, 512:768] = spread_ref[...]
    penalty = coeffs_ref[:, 0:1]
    metric = metric_ref[...]
    node, level = coupling_matrices(node_ref, level_ref)
    weights_ref[:, 0:256] = node
    weights_ref[:, 256:512] = level
    low_node = low_node_matrix(node_ref[0])
    low_node_ref[...] = low_node
    factor = diagonal(metric, penalty)
    pack_sides(state_ref, penalty, edges)
    lowest = jnp.concatenate([whole_rows(state_ref, 256 * v, 16) for v in range(4)], axis=0)
    high, low = [dot(select_low, part).astype(BF16) for part in halves(penalty * lowest)]
    here_low_ref[0:16, :] = high[0:16]
    here_low_ref[16:32, :] = low[0:16]
    away_low_ref[0:16, :] = high[16:32]
    away_low_ref[16:32, :] = low[16:32]
    edges[256:272, 0:512] = high[32:48]
    edges[256:272, 512:1024] = high[48:64]
    edges[272:288, 0:512] = low[32:48]
    edges[272:288, 512:1024] = low[48:64]
    moved = dot(edges[...], inner_ref[...]).astype(BF16)
    rate = exchange_rate(coeffs_ref, mask_ref[0])
    rates = jnp.concatenate([rate] * 4, axis=0)
    forced = rates * jnp.concatenate([forcing_ref[0, v] for v in range(4)], axis=0)
    factor_low = factor - rate
    factor_ref[...] = factor_low
    scalars.wait()
    mixed = mix_to_lowest(level_smem, state_ref)
    near = moved[256:288]
    p_low = jnp.concatenate([factor_low] * 4, axis=0) * lowest + forced + mixed
    p_low = p_low + low_node_product(low_node, lowest * metric)
    p_low = p_low + dot(spread_inner, jnp.concatenate([near[:, 0:512], near[:, 512:1024]], axis=0))
    low_ref[...] = p_low
    high, low = [dot(select_low[0:32], part).astype(BF16) for part in halves(penalty * (p_low + mixed))]
    here_low_ref[32:48, :] = high[0:16]
    here_low_ref[48:64, :] = low[0:16]
    away_low_ref[32:48, :] = high[16:32]
    away_low_ref[48:64, :] = low[16:32]
    factors = levels_of(factor)
    for v in range(4):
        u = whole_rows(state_ref, 256 * v, 256)
        operand = [(u * metric).astype(BF16), u.astype(BF16)]
        operand += [moved[64 * v : 64 * (v + 1), 512 * side : 512 * (side + 1)] for side in range(2)]
        p = dot(jnp.concatenate([weights_ref[:, 0:512], weights_ref[:, 640:768]], axis=1), jnp.concatenate(operand, axis=0))
        p = jnp.concatenate([p_low[16 * v : 16 * (v + 1)], (factors * u + p)[16:256]], axis=0)
        for c in range(4):
            part_ref[c, 256 * v : 256 * (v + 1), :] = p[:, LANES[c]]
    pack_facing(part_ref, penalty, here_ref, away_ref, 0)
    mixed = mix_to_lowest(level_smem, part_ref)
    node_at = iota((64, 1), 0) % 16
    facing = jnp.where((node_at // 4 == 0) | (node_at // 4 == 3), penalty * penalty, 0.0)
    base_ref[...] = mixed + forced + facing * lowest


def lowest_kernel(
    low_ref, base_ref, factor_ref, low_node_ref, metric_ref, coeffs_ref, away_ref, here_ref, here_map, away_map, inner_ref,
    surface_ref,
):
    penalty = coeffs_ref[:, 0:1]
    here = dot(here_ref[...], here_map[...]).astype(BF16)
    away = dot(away_ref[...], away_map[...]).astype(BF16)
    outer, inner, select = low_spread(0, 1), low_spread(2, 3), low_select()
    u1 = low_ref[...] + dot(outer, jnp.concatenate([here[0:32], away[0:32]], axis=0))
    high, low = [dot(select[32:64], part).astype(BF16) for part in halves(penalty * u1)]
    sides = [jnp.concatenate([high[at : at + 16], low[at : at + 16]], axis=0) for at in (0, 16)]
    near = dot(jnp.concatenate(sides, axis=1), inner_ref[...]).astype(BF16)
    x = base_ref[...] + jnp.concatenate([factor_ref[...]] * 4, axis=0) * u1
    x = x + low_node_product(low_node_ref[...], u1 * metric_ref[...])
    x = x + dot(outer, jnp.concatenate([here[32:64], away[32:64]], axis=0))
    x = x + dot(inner, jnp.concatenate([near[:, 0:512], near[:, 512:1024]], axis=0))
    x = x.astype(BF16)
    for v in range(4):
        for q in range(4):
            surface_ref[64 * v + 16 * q : 64 * v + 16 * (q + 1), :] = x[16 * v : 16 * (v + 1), 128 * q : 128 * (q + 1)]


def tables_kernel(
    partner_ref, rows_ref, cols_ref, order_ref, first_ref, here_map, away_map, pick_ref, sum_ref,
):
    last = ends()[0] == 12
    before, after = partner_ref[0:1, 0:512], partner_ref[0:1, 1536:2048] - 2560
    here_map[...] = jnp.where(iota((512, 512), 0) == jnp.where(last, after, before), 1.0, 0.0).astype(BF16)
    away_map[...] = jnp.where(iota((512, 512), 0) == jnp.where(last, before, after), 1.0, 0.0).astype(BF16)
    odd = lax.rem(lax.axis_index("tile"), 2)
    slots = rows_ref.shape[1]
    wide = 4 * slots
    repeat = (iota((slots, wide), 1) // 4 == iota((slots, wide), 0)).astype(BF16)
    widen = lambda ref: dot(jnp.broadcast_to(ref[0:1, :].astype(BF16), (16, slots)), repeat)[0:1].astype(jnp.int32)
    rows, cols = widen(rows_ref), widen(cols_ref)
    tile, block = cols // 64, cols % 64
    tile = jnp.where(odd == 1, 2 - tile, tile)
    var = iota((1, wide), 1) % 4
    wanted = tile * 256 + var * 64 + (block % 4) * 16 + block // 4
    pick_ref[...] = jnp.transpose((iota((768, wide), 0) == wanted).astype(F32)).astype(BF16)
    wanted = jnp.where(rows == 64, -1, var * 64 + (rows % 4) * 16 + rows // 4)
    sum_ref[...] = (iota((256, wide), 0) == wanted).astype(BF16)


def finish_kernel(
    state_ref, part_ref, away_first, here_first, away_ref, here_ref, here_map, away_map, inner_ref, weights_ref,
    metric_ref, coeffs_ref, mask_ref, forcing_ref,
    next_hbm, middle_ref, next_ref, edges, sems,
):
    penalty = coeffs_ref[:, 0:1]
    metric = metric_ref[...]
    here = dot(jnp.concatenate([here_first[...], here_ref[...]], axis=0), here_map[...]).astype(BF16)
    away = dot(jnp.concatenate([away_first[...], away_ref[...]], axis=0), away_map[...]).astype(BF16)
    for v in range(4):
        rows = slice(64 * v, 64 * (v + 1))
        halo = dot(weights_ref[:, 512:640], jnp.concatenate([here[rows], away[rows]], axis=0))
        for c in range(4):
            middle_ref[c, 256 * v : 256 * (v + 1), :] = part_ref[c, 256 * v : 256 * (v + 1), :] + halo[:, LANES[c]]
    pack_sides(middle_ref, penalty, edges)
    moved = dot(edges[...], inner_ref[...]).astype(BF16)
    factors = levels_of(diagonal(metric, penalty))
    node = iota((256, 1), 0) % 16
    facing = jnp.where((node // 4 == 0) | (node // 4 == 3), penalty * penalty, 0.0)
    rate = exchange_rate(coeffs_ref, mask_ref[0])
    copies = []
    for v in range(4):
        u1 = whole_rows(middle_ref, 256 * v, 256)
        rows = slice(64 * v, 64 * (v + 1))
        far = slice(256 + 64 * v, 256 + 64 * (v + 1))
        operand = [(u1 * metric).astype(BF16), u1.astype(BF16), here[far], away[far]]
        operand += [moved[rows, 512 * side : 512 * (side + 1)] for side in range(2)]
        x = factors * u1 + facing * whole_rows(state_ref, 256 * v, 256)
        x = x + dot(weights_ref[...], jnp.concatenate(operand, axis=0))
        added = rate * (forcing_ref[0, v] - u1[0:16])
        next_ref[256 * v : 256 * (v + 1), :] = jnp.concatenate([x[0:16] + added, x[16:256]], axis=0)
        rows = pl.ds(256 * v, 256)
        copies.append(pltpu.make_async_copy(next_ref.at[rows], next_hbm.at[rows], sems.at[v]))
        copies[-1].start()
    for copy in copies:
        copy.wait()


def remap_kernel(far_ref, near_ref, own_ref, pick_ref, sum_ref, blocks_ref, out_ref, products):
    picked = dot(pick_ref[:, 0:256], far_ref[...])
    picked = picked + dot(pick_ref[:, 256:512], own_ref[...])
    picked = picked + dot(pick_ref[:, 512:768], near_ref[...])
    slots = blocks_ref.shape[0]
    for quad in range(slots // 4):
        part = picked[16 * quad : 16 * (quad + 1)]
        upper = iota((16, 1), 0) % 8 < 4
        left = jnp.concatenate([jnp.where(upper, part, 0.0), jnp.where(upper, 0.0, part)], axis=1).astype(BF16)
        right = [jnp.concatenate([blocks_ref[4 * quad + 2 * h], blocks_ref[4 * quad + 2 * h + 1]], axis=1) for h in range(2)]
        both = lax.dot_general(
            left, jnp.concatenate(right, axis=0), (((1,), (1,)), ((), ())), preferred_element_type=F32
        )
        products[16 * quad : 16 * quad + 8, :] = both[0:8, 0:128]
        products[16 * quad + 8 : 16 * (quad + 1), :] = both[8:16, 128:256]
    value = products[...]
    high = value.astype(BF16)
    low = (value - high.astype(F32)).astype(BF16)
    total = dot(sum_ref[...], high) + dot(sum_ref[...], low)
    for v in range(4):
        for q in range(4):
            out_ref[0, v, :, 128 * q : 128 * (q + 1)] = total[64 * v + 16 * q : 64 * v + 16 * (q + 1)]


def call(kernel, outs, scratch=(), inputs="", results="", aliases={}, cost=0):
    spaces = {"v": pltpu.VMEM, "s": pltpu.SMEM, "h": pltpu.HBM, "a": pl.ANY}
    place = lambda kind: pl.BlockSpec(memory_space=spaces[kind])
    results = results or "v" * len(outs)
    return pl.pallas_call(
        kernel,
        out_shape=[jax.ShapeDtypeStruct(shape, kind) for shape, kind in outs],
        in_specs=[place(kind) for kind in inputs],
        out_specs=[place(kind) for kind in results],
        input_output_aliases=aliases,
        scratch_shapes=list(scratch),
        cost_estimate=pl.CostEstimate(flops=cost, bytes_accessed=0, transcendentals=0) if cost else None,
        compiler_params=pltpu.CompilerParams(vmem_limit_bytes=VMEM_LIMIT),
    )


def shards(
    state, metric, element_coupling, level_coupling, coeffs, edge_partner, sea_mask, forcing,
    remap_weights, remap_rows, remap_cols,
):
    tiles = lax.axis_size("tile")
    here = [(t, t ^ 1) for t in range(tiles)]
    away = [(t, (t + 1) % tiles if t % 2 else (t - 1) % tiles) for t in range(tiles)]
    crossed = lambda pairs: [(c * tiles + a, (1 - c) * tiles + b) for c in range(2) for a, b in pairs]
    straight = [(t, t) for t in range(tiles)]
    flat = state.reshape(1024, 512)
    hbm = lambda *values: [pltpu.with_memory_space_constraint(value, pltpu.HBM) for value in values]
    chunks, here_first, away_first, inner, spread = call(
        first_kernel,
        [((4, 1024, 128), F32), ((256, 512), BF16), ((256, 512), BF16), ((1024, 1024), BF16), ((256, 256), BF16)],
        [pltpu.VMEM(edge_partner.shape, jnp.int32), pltpu.SMEM(coeffs.shape, F32), pltpu.SemaphoreType.DMA((6,))],
        "hhh",
    )(*hbm(flat, edge_partner, coeffs))
    away_first = lax.ppermute(away_first, "tile", away)
    here_first = lax.ppermute(here_first, "tile", here)
    inputs = (metric, element_coupling, level_coupling, coeffs, sea_mask, forcing)
    (part, here_edge, away_edge, here_low, away_low, weights, low, base, factor, low_node) = call(
        local_kernel,
        [
            ((4, 1024, 128), F32), ((256, 512), BF16), ((256, 512), BF16), ((64, 512), BF16),
            ((64, 512), BF16), ((256, 768), BF16),
            ((64, 512), F32), ((64, 512), F32), ((16, 512), F32), ((64, 192), BF16),
        ],
        [pltpu.SMEM((1, 16, 16), F32), pltpu.VMEM((288, 1024), BF16), pltpu.SemaphoreType.DMA],
        "v" * 9 + "a",
    )(chunks, inner, spread, *inputs, here_first)
    away_low = lax.ppermute(away_low, "tile", away)
    here_low = lax.ppermute(here_low, "tile", here)
    away_edge = lax.ppermute(away_edge, "tile", away)
    here_edge = lax.ppermute(here_edge, "tile", here)
    slots = remap_rows.shape[1]
    here_map, away_map, pick, total = call(
        tables_kernel,
        [
            ((512, 512), BF16), ((512, 512), BF16), ((4 * slots, 768), BF16), ((256, 4 * slots), BF16),
        ],
        inputs="vvvaa", results="vvvv", cost=4000000000,
    )(edge_partner, remap_rows, remap_cols, here_edge, away_first)
    (surface,) = call(lowest_kernel, [((256, 128), BF16)], inputs="v" * 11, cost=40000000000)(
        low, base, factor, low_node, metric, coeffs, away_low, here_low, here_map, away_map, inner
    )
    far = lax.ppermute(surface, ("comp", "tile"), crossed(away))
    near = lax.ppermute(surface, ("comp", "tile"), crossed(here))
    own = lax.ppermute(surface, ("comp", "tile"), crossed(straight))
    (nxt,) = call(
        finish_kernel,
        [((1024, 512), F32)],
        [
            pltpu.VMEM((4, 1024, 128), F32), pltpu.VMEM((1024, 512), F32), pltpu.VMEM((256, 1024), BF16),
            pltpu.SemaphoreType.DMA((4,)),
        ],
        "v" * 14, "h",
    )(chunks, part, away_first, here_first, away_edge, here_edge, here_map, away_map, inner, weights, metric, coeffs, sea_mask, forcing)
    (new_forcing,) = call(
        remap_kernel, [(forcing.shape, F32)], [pltpu.VMEM((4 * slots, 128), F32)], "v" * 6,
    )(far, near, own, pick, total, remap_weights[0])
    return nxt.reshape(state.shape), new_forcing


def solution(mesh):
    placed = (
        P("comp", None, None, None, "tile"),
        P("comp", "tile"),
        P("comp", None, None),
        P("comp", None, None),
        P("comp", None),
        P("comp", "tile"),
        P("comp", None, "tile"),
        P("comp", None, None, "tile"),
        P("comp", "tile", None, None),
        P("comp", "tile"),
        P("comp", "tile"),
    )
    return jax.shard_map(
        shards,
        mesh=mesh,
        in_specs=placed,
        out_specs=(P("comp", None, None, None, "tile"), P("comp", None, None, "tile")),
        check_vma=False,
    )
```
